32 devices in a mesh: blk: 8 (over z, y), row: 4 (over x, core).
Axes of the slice: x: 2, y: 2, z: 4, core: 2. Of those that a mesh axis runs over, the one named last changes fastest.
Arguments:
- pool_embeds: bfloat16 [8192, 768], P('blk'), may hold values from -24 to 24
- target_samples: bfloat16 [2048, 768], P(('blk', 'row')), may hold values from -6 to 6
- reference_samples: bfloat16 [2048, 768], P(('blk', 'row')), may hold values from -6 to 6
Outputs:
- log_ratio: float32 [8192], P('blk')
- standardized: float32 [8192], P('blk')
The draws below stay inside these ranges and needn't reach their ends.
All inputs are finite; a program needn't handle non-finite values.
Results may differ from the reference program's by a relative error of at most 0.0003.
Values may be sent and summed in bfloat16 or wider, within the bound.
A program may use at most 128 MiB of HBM per device.

```python
import jax
import jax.numpy as jnp
from jax import lax

D = 768
NPOOL = 8192
NSAMP = 2048


def sample_set(key, set_index):
    local_key = jax.random.fold_in(key, 101 + set_index)
    normal_key, pick_key, extra_key = jax.random.split(local_key, 3)
    spread_scale = 1.0 + 0.15 * set_index
    pick_draw = jax.random.randint(pick_key, (NSAMP,), 0, 32)
    forced = jax.random.randint(extra_key, (), 0, NSAMP)
    chosen = (pick_draw == 0) | (jnp.arange(NSAMP, dtype=jnp.int32) == forced)
    factor = jnp.where(chosen, 2.2, 1.0).astype(jnp.float32)
    raw_values = jax.random.normal(normal_key, (NSAMP, D), jnp.float32)
    values = jnp.clip(raw_values * spread_scale * factor[:, None], -6.0, 6.0)
    return (values, chosen)


def copy_rows(samples, chosen, row_picks):
    flags = 1 - chosen.astype(jnp.int32)
    sorted_rows = jnp.argsort(flags, stable=True)
    chosen_count = jnp.maximum(jnp.sum(chosen.astype(jnp.int32)), 1)
    return samples[sorted_rows[row_picks % chosen_count]]


def draw_target_samples(key, part):
    values, chosen = sample_set(key, 0)
    return values.astype(jnp.bfloat16)


def draw_reference_samples(key, part):
    values, chosen = sample_set(key, 1)
    return values.astype(jnp.bfloat16)


def draw_pool_embeds(key, part):
    first_key, second_key = jax.random.split(key)
    kind_key = jax.random.fold_in(key, 201)
    choose_key = jax.random.fold_in(key, 202)
    noise_key = jax.random.fold_in(key, 203)
    base = jnp.clip(jax.random.normal(first_key, (NPOOL, D), jnp.float32), -6.0, 6.0)
    position = jnp.arange(NPOOL, dtype=jnp.float32) / NPOOL
    row_scale = jax.random.uniform(second_key, (NPOOL, 1), jnp.float32, 0.6, 1.4)
    base_rows = base * row_scale * (0.7 + 0.6 * position[:, None])
    target_set, target_chosen = sample_set(key, 0)
    ref_set, ref_chosen = sample_set(key, 1)
    row_kind = jax.random.randint(kind_key, (NPOOL,), 0, 64)
    row_picks = jax.random.randint(choose_key, (NPOOL,), 0, 1 << 20)
    near_target = copy_rows(target_set, target_chosen, row_picks)
    near_ref = copy_rows(ref_set, ref_chosen, row_picks)
    noise = 0.3 * jnp.clip(jax.random.normal(noise_key, (NPOOL, D), jnp.float32), -6.0, 6.0)
    mixed = jnp.where(row_kind[:, None] == 0, near_target + noise, jnp.where(row_kind[:, None] == 1, near_ref + noise, base_rows))
    return mixed.astype(jnp.bfloat16)


def setup_inputs(seed: int = 0) -> dict:
    splits = jax.random.split(jax.random.key(seed), 4)
    pool_embeds = draw_pool_embeds(jax.random.fold_in(splits[3], 71), 0)
    target_samples = draw_target_samples(jax.random.fold_in(splits[3], 71), 0)
    reference_samples = draw_reference_samples(jax.random.fold_in(splits[3], 71), 0)
    return dict(pool_embeds=pool_embeds, target_samples=target_samples, reference_samples=reference_samples)


KERNEL_GAIN = 30.0

def log_density(pool_rows, samples, sample_norms):
    pool_norms = lax.optimization_barrier(jnp.sum(jnp.square(pool_rows.astype(jnp.float32)), axis=1))
    products = jnp.dot(pool_rows, samples.T, preferred_element_type=jnp.float32)
    scores = (2.0 * products - pool_norms[:, None] - sample_norms[None, :]) * (KERNEL_GAIN / D)
    return jax.nn.logsumexp(scores, axis=1)

def reference(pool_embeds, target_samples, reference_samples):
    target_norms = lax.optimization_barrier(jnp.sum(jnp.square(target_samples.astype(jnp.float32)), axis=1))
    ref_norms = lax.optimization_barrier(jnp.sum(jnp.square(reference_samples.astype(jnp.float32)), axis=1))
    blocked = pool_embeds.reshape(NPOOL // 256, 256, D)

    def per_block(pool_rows):
        return log_density(pool_rows, target_samples, target_norms) - log_density(pool_rows, reference_samples, ref_norms)
    log_ratio = lax.map(per_block, blocked).reshape(NPOOL)
    mean_value = jnp.sum(log_ratio) / NPOOL
    variance = jnp.sum(jnp.square(log_ratio - mean_value)) / NPOOL
    standardized = (log_ratio - mean_value) / jnp.sqrt(variance + 1e-05)
    return (log_ratio, standardized)
```

```python
import functools

import jax
import jax.numpy as jnp
from jax import lax
from jax.experimental import pallas as pl
from jax.experimental.pallas import tpu as pltpu
from jax.sharding import PartitionSpec as P

KERNEL_GAIN = 30.0
MESH = pl.DeviceIdType.MESH


def density_kernel(
    n_blk,
    n_row,
    pool_hbm,
    target_hbm,
    ref_hbm,
    ratio_out,
    std_out,
    pool,
    gathered,
    pool_norms,
    high,
    total,
    partials,
    stats,
    load_sem,
    right_send,
    left_send,
    line_recv,
    side_send,
    side_recv,
    row_send,
    row_recv,
    stat_send,
    stat_recv,
):
    me = lax.axis_index("blk")
    my_row = lax.axis_index("row")
    length = n_blk // 2
    place = me // 2
    side = lax.rem(me, 2)
    other = me + 1 - 2 * side
    rows, depth = pool.shape
    width = target_hbm.shape[0]
    factor = KERNEL_GAIN / depth
    sources = (target_hbm, ref_hbm)
    nt = (((1,), (1,)), ((), ()))

    pool_load = pltpu.make_async_copy(pool_hbm, pool, load_sem.at[2])
    pool_load.start()
    own_loads = [
        pltpu.make_async_copy(sources[k], gathered.at[place, k, side], load_sem.at[k]) for k in range(2)
    ]
    for load in own_loads:
        load.start()

    barrier = pltpu.get_barrier_semaphore()

    def greet(i, carry):
        pl.semaphore_signal(barrier, inc=1, device_id={"blk": lax.rem(me + i, n_blk)}, device_id_type=MESH)
        return carry

    lax.fori_loop(1, n_blk, greet, 0)
    for i in range(1, n_row):
        pl.semaphore_signal(barrier, inc=1, device_id={"row": lax.rem(my_row + i, n_row)}, device_id_type=MESH)
    pl.semaphore_wait(barrier, n_blk - 1 + n_row - 1)

    def line_copy(origin, k, src, step, sems):
        return pltpu.make_async_remote_copy(
            src_ref=src,
            dst_ref=gathered.at[origin, k, side],
            send_sem=sems.at[origin, k],
            recv_sem=line_recv.at[origin, k],
            device_id={"blk": me + 2 * step},
            device_id_type=MESH,
        )

    def side_copy(origin, k, src, to_side):
        return pltpu.make_async_remote_copy(
            src_ref=src,
            dst_ref=gathered.at[origin, k, to_side],
            send_sem=side_send.at[origin, k],
            recv_sem=side_recv.at[origin, k],
            device_id={"blk": other},
            device_id_type=MESH,
        )

    for k in range(2):

        @pl.when(place < length - 1)
        def _(k=k):
            line_copy(place, k, sources[k], 1, right_send).start()

        @pl.when(place > 0)
        def _(k=k):
            line_copy(place, k, sources[k], -1, left_send).start()

        side_copy(place, k, sources[k], side).start()

    pool_load.wait()
    ones = jnp.ones((8, depth), jnp.bfloat16)
    tile = 256 if rows % 256 == 0 else rows

    def norm_tile(i, carry):
        at = pl.multiple_of(i * tile, tile)
        squares = jnp.square(pool[pl.ds(at, tile), :].astype(jnp.float32))
        coarse = squares.astype(jnp.bfloat16)
        fine = (squares - coarse.astype(jnp.float32)).astype(jnp.bfloat16)
        sums = lax.dot_general(ones, coarse, nt, preferred_element_type=jnp.float32)
        sums = sums + lax.dot_general(ones, fine, nt, preferred_element_type=jnp.float32)
        pool_norms[:, pl.ds(at, tile)] = sums[0:1, :] * factor
        return carry

    lax.fori_loop(0, rows // tile, norm_tile, 0)
    high[...] = jnp.full_like(high, -1e30)
    total[...] = jnp.zeros_like(total)
    for load in own_loads:
        load.wait()

    def fold(origin):
        for k in range(2):
            side_copy(origin, k, gathered.at[origin, k, 1 - side], 1 - side).wait_recv()
        block = gathered[origin].reshape(4 * width, depth)
        norms = jnp.sum(jnp.square(block.astype(jnp.float32)), axis=1, keepdims=True)
        products = lax.dot_general(block, pool[...], nt, preferred_element_type=jnp.float32)
        scores_all = (2.0 * products - norms) * factor
        for k in range(2):
            scores = scores_all[2 * width * k : 2 * width * (k + 1), :]
            old = high[k : k + 1, :]
            new = jnp.maximum(old, jnp.max(scores, axis=0, keepdims=True))
            summed = jnp.sum(jnp.exp(scores - new), axis=0, keepdims=True)
            total[k : k + 1, :] = total[k : k + 1, :] * jnp.exp(old - new) + summed
            high[k : k + 1, :] = new

    def fold_step(step):
        @pl.when(place >= step)
        def _():
            fold(place - step)

        @pl.when((step > 0) & (place + step < length))
        def _():
            fold(place + step)

    def relay(step, carry):
        for k in range(2):

            @pl.when(place >= step)
            def _(k=k):
                origin = place - step
                block = gathered.at[origin, k, side]
                line_copy(origin, k, block, 1, right_send).wait_recv()

                @pl.when(place < length - 1)
                def _():
                    line_copy(origin, k, block, 1, right_send).start()

                side_copy(origin, k, block, side).start()

            @pl.when(place + step < length)
            def _(k=k):
                origin = place + step
                block = gathered.at[origin, k, side]
                line_copy(origin, k, block, -1, left_send).wait_recv()

                @pl.when(place > 0)
                def _():
                    line_copy(origin, k, block, -1, left_send).start()

                side_copy(origin, k, block, side).start()

        fold_step(step - 1)
        return carry

    lax.fori_loop(1, length, relay, 0)
    fold_step(length - 1)

    partials[my_row] = high[...] + jnp.log(total[...])

    def row_copy(slot, peer):
        return pltpu.make_async_remote_copy(
            src_ref=partials.at[slot],
            dst_ref=partials.at[slot],
            send_sem=row_send.at[peer],
            recv_sem=row_recv.at[slot],
            device_id={"row": peer},
            device_id_type=MESH,
        )

    peers = [lax.rem(my_row + i, n_row) for i in range(1, n_row)]
    for peer in peers:
        row_copy(my_row, peer).start()
    for peer in peers:
        row_copy(peer, peer).wait_recv()
    parts = [partials[i] for i in range(n_row)]
    top = functools.reduce(jnp.maximum, parts)
    mass = functools.reduce(jnp.add, [jnp.exp(part - top) for part in parts])
    logs = top + jnp.log(mass) - pool_norms[...]
    ratio = logs[0:1, :] - logs[1:2, :]
    ratio_out[...] = ratio

    local_mean = jnp.sum(ratio, axis=1, keepdims=True) / rows
    local_spread = jnp.sum(jnp.square(ratio - local_mean), axis=1, keepdims=True)
    lanes = stats.shape[2]
    stats[me, 0:1, :] = jnp.broadcast_to(local_mean, (1, lanes))
    stats[me, 1:2, :] = jnp.broadcast_to(local_spread, (1, lanes))

    def stat_copy(slot, peer):
        return pltpu.make_async_remote_copy(
            src_ref=stats.at[slot],
            dst_ref=stats.at[slot],
            send_sem=stat_send.at[peer],
            recv_sem=stat_recv.at[slot],
            device_id={"blk": peer},
            device_id_type=MESH,
        )

    def stat_start(i, carry):
        stat_copy(me, lax.rem(me + i, n_blk)).start()
        return carry

    def stat_wait(i, carry):
        peer = lax.rem(me + i, n_blk)
        stat_copy(peer, peer).wait_recv()
        return carry

    lax.fori_loop(1, n_blk, stat_start, 0)

    for k in range(2):

        def sent(origin, carry, k=k):
            @pl.when((origin <= place) & (place < length - 1))
            def _():
                line_copy(origin, k, gathered.at[origin, k, side], 1, right_send).wait_send()

            @pl.when((origin >= place) & (place > 0))
            def _():
                line_copy(origin, k, gathered.at[origin, k, side], -1, left_send).wait_send()

            side_copy(origin, k, gathered.at[origin, k, side], side).wait_send()
            return carry

        lax.fori_loop(0, length, sent, 0)
    for peer in peers:
        row_copy(my_row, peer).wait_send()

    lax.fori_loop(1, n_blk, stat_wait, 0)
    means = stats[:, 0, :]
    spreads = stats[:, 1, :]
    mean = jnp.sum(means, axis=0, keepdims=True) / n_blk
    spread = jnp.sum(spreads, axis=0, keepdims=True)
    spread = spread + rows * jnp.sum(jnp.square(means - mean), axis=0, keepdims=True)
    scale = jnp.sqrt(spread / (rows * n_blk) + 1e-05)
    std_out[...] = (ratio_out[...] - mean[:, 0:1]) / scale[:, 0:1]

    def stat_sent(i, carry):
        stat_copy(me, lax.rem(me + i, n_blk)).wait_send()
        return carry

    lax.fori_loop(1, n_blk, stat_sent, 0)


def body(n_blk, n_row, pool_embeds, target_samples, reference_samples):
    rows, depth = pool_embeds.shape
    width = target_samples.shape[0]
    length = n_blk // 2
    dma = pltpu.SemaphoreType.DMA
    flops = 2 * rows * depth * 2 * width * n_blk
    ratio, standardized = pl.pallas_call(
        functools.partial(density_kernel, n_blk, n_row),
        out_shape=[jax.ShapeDtypeStruct((1, rows), jnp.float32)] * 2,
        in_specs=[pl.BlockSpec(memory_space=pl.ANY)] * 3,
        out_specs=[pl.BlockSpec(memory_space=pltpu.VMEM)] * 2,
        scratch_shapes=[
            pltpu.VMEM((rows, depth), jnp.bfloat16),
            pltpu.VMEM((length, 2, 2, width, depth), jnp.bfloat16),
            pltpu.VMEM((1, rows), jnp.float32),
            pltpu.VMEM((2, rows), jnp.float32),
            pltpu.VMEM((2, rows), jnp.float32),
            pltpu.VMEM((n_row, 2, rows), jnp.float32),
            pltpu.VMEM((n_blk, 2, 128), jnp.float32),
            dma((3,)),
            dma((length, 2)),
            dma((length, 2)),
            dma((length, 2)),
            dma((length, 2)),
            dma((length, 2)),
            dma((n_row,)),
            dma((n_row,)),
            dma((n_blk,)),
            dma((n_blk,)),
        ],
        compiler_params=pltpu.CompilerParams(
            collective_id=0, has_side_effects=True, vmem_limit_bytes=62 * 1024 * 1024
        ),
        cost_estimate=pl.CostEstimate(flops=flops, bytes_accessed=2 * rows * depth, transcendentals=0),
    )(pool_embeds, target_samples, reference_samples)
    return ratio.reshape(rows), standardized.reshape(rows)


def solution(mesh):
    in_specs = (P("blk", None), P(("blk", "row"), None), P(("blk", "row"), None))
    out_specs = (P("blk"), P("blk"))
    part = functools.partial(body, mesh.shape["blk"], mesh.shape["row"])
    return jax.shard_map(part, mesh=mesh, in_specs=in_specs, out_specs=out_specs, check_vma=False)
```

```python
import functools
import math

import jax
import jax.numpy as jnp
from jax import lax
from jax.experimental import pallas as pl
from jax.experimental.pallas import tpu as pltpu
from jax.sharding import PartitionSpec as P

KERNEL_GAIN = 30.0
LOG2E = math.log2(math.e)
LN2 = math.log(2.0)
CHUNKS = 4
MESH = pl.DeviceIdType.MESH


def density_kernel(
    n_blk,
    n_row,
    pool_hbm,
    target_hbm,
    ref_hbm,
    logs_out,
    mean_out,
    scale_out,
    pool,
    other_pool,
    gathered,
    pool_norms,
    high,
    total,
    partials,
    outgoing,
    stats,
    load_sem,
    right_send,
    left_send,
    line_recv,
    cross_send,
    x_send,
    core_send,
    pool_recv,
    row_send,
    side_send,
    part_recv,
    stat_send,
    stat_recv,
):
    me = lax.axis_index("blk")
    my_row = lax.axis_index("row")
    length = n_blk // 2
    place = me // 2
    other = me + 1 - 2 * lax.rem(me, 2)
    core = lax.rem(my_row, 2)
    core_peer = my_row + 1 - 2 * core
    x_peers = [lax.rem(my_row + 2 * j, n_row) for j in range(1, n_row // 2)]
    row_peers = [lax.rem(my_row + i, n_row) for i in range(1, n_row)]
    rows, depth = pool.shape
    width = target_hbm.shape[0]
    chunk = other_pool.shape[2]
    factor = KERNEL_GAIN / depth * LOG2E
    sources = (target_hbm, ref_hbm)
    nt = (((1,), (1,)), ((), ()))

    pool_load = pltpu.make_async_copy(pool_hbm, pool, load_sem.at[2])
    pool_load.start()
    own_loads = [
        pltpu.make_async_copy(sources[k], gathered.at[place, k], load_sem.at[k]) for k in range(2)
    ]
    for load in own_loads:
        load.start()

    barrier = pltpu.get_barrier_semaphore()

    def greet(i, carry):
        pl.semaphore_signal(barrier, inc=1, device_id={"blk": lax.rem(me + i, n_blk)}, device_id_type=MESH)
        return carry

    lax.fori_loop(1, n_blk, greet, 0)
    for peer in row_peers:
        pl.semaphore_signal(barrier, inc=1, device_id={"row": peer}, device_id_type=MESH)
        pl.semaphore_signal(barrier, inc=1, device_id={"blk": other, "row": peer}, device_id_type=MESH)
    pl.semaphore_wait(barrier, n_blk - 1 + 2 * (n_row - 1))

    def line_copy(origin, k, src, step, sems):
        return pltpu.make_async_remote_copy(
            src_ref=src,
            dst_ref=gathered.at[origin, k],
            send_sem=sems.at[origin, k],
            recv_sem=line_recv.at[origin, k],
            device_id={"blk": me + 2 * step},
            device_id_type=MESH,
        )

    def cross_copy(c):
        at = pl.multiple_of((my_row * CHUNKS + c) * chunk, chunk)
        return pltpu.make_async_remote_copy(
            src_ref=pool_hbm.at[pl.ds(at, chunk)],
            dst_ref=other_pool.at[my_row, c],
            send_sem=cross_send.at[c],
            recv_sem=pool_recv.at[my_row, c],
            device_id={"blk": other},
            device_id_type=MESH,
        )

    def row_relay(quarter, c, peer, send_sem):
        return pltpu.make_async_remote_copy(
            src_ref=other_pool.at[quarter, c],
            dst_ref=other_pool.at[quarter, c],
            send_sem=send_sem,
            recv_sem=pool_recv.at[quarter, c],
            device_id={"row": peer},
            device_id_type=MESH,
        )

    def core_copy(quarter, c):
        return row_relay(quarter, c, core_peer, core_send.at[quarter, c])

    def x_copy(c, peer):
        return row_relay(my_row, c, peer, x_send.at[peer, c])

    for k in range(2):

        @pl.when(place < length - 1)
        def _(k=k):
            line_copy(place, k, sources[k], 1, right_send).start()

        @pl.when(place > 0)
        def _(k=k):
            line_copy(place, k, sources[k], -1, left_send).start()

    for c in range(CHUNKS):
        cross_copy(c).start()

    high[...] = jnp.full_like(high, -1e30)
    total[...] = jnp.zeros_like(total)

    def fold(origin, which):
        block = gathered[origin].reshape(2 * width, depth)
        columns = pool[...] if which == 0 else other_pool[...].reshape(rows, depth)
        norms = jnp.sum(jnp.square(block.astype(jnp.float32)), axis=1, keepdims=True) * factor
        products = lax.dot_general(block, columns, nt, preferred_element_type=jnp.float32)
        scores_all = products * (2.0 * factor) - norms
        for k in range(2):
            scores = scores_all[width * k : width * (k + 1), :]
            at = 2 * which + k
            old = high[at : at + 1, :]
            new = jnp.maximum(old, jnp.max(scores, axis=0, keepdims=True))
            summed = jnp.sum(jnp.exp2(scores - new), axis=0, keepdims=True)
            total[at : at + 1, :] = total[at : at + 1, :] * jnp.exp2(old - new) + summed
            high[at : at + 1, :] = new

    pool_load.wait()
    for load in own_loads:
        load.wait()
    fold(place, 0)

    ones = jnp.ones((8, depth), jnp.bfloat16)
    tile = 256 if rows % 256 == 0 else rows

    def norm_tile(i, carry):
        at = pl.multiple_of(i * tile, tile)
        squares = jnp.square(pool[pl.ds(at, tile), :].astype(jnp.float32))
        coarse = squares.astype(jnp.bfloat16)
        fine = (squares - coarse.astype(jnp.float32)).astype(jnp.bfloat16)
        sums = lax.dot_general(ones, coarse, nt, preferred_element_type=jnp.float32)
        sums = sums + lax.dot_general(ones, fine, nt, preferred_element_type=jnp.float32)
        pool_norms[:, pl.ds(at, tile)] = sums[0:1, :] * factor
        return carry

    line_ticks = 2 * (length - 1)
    ticks = max(line_ticks, CHUNKS + 2)

    def tick(i, carry):
        step = i // 2 + 1
        k = lax.rem(i, 2)

        @pl.when((i < line_ticks) & (place >= step))
        def _():
            origin = place - step
            block = gathered.at[origin, k]
            line_copy(origin, k, block, 1, right_send).wait_recv()

            @pl.when(place < length - 1)
            def _():
                line_copy(origin, k, block, 1, right_send).start()

        @pl.when((i < line_ticks) & (place + step < length))
        def _():
            origin = place + step
            block = gathered.at[origin, k]
            line_copy(origin, k, block, -1, left_send).wait_recv()

            @pl.when(place > 0)
            def _():
                line_copy(origin, k, block, -1, left_send).start()

        @pl.when(i < CHUNKS)
        def _():
            cross_copy(i).wait_recv()
            for peer in x_peers:
                x_copy(i, peer).start()
            core_copy(my_row, i).start()

        @pl.when((i >= 1) & (i <= CHUNKS))
        def _():
            for peer in x_peers:
                row_relay(peer, i - 1, peer, x_send.at[peer, i - 1]).wait_recv()
                core_copy(peer, i - 1).start()

        @pl.when(i < rows // tile)
        def _():
            norm_tile(i, 0)

        @pl.when((k == 1) & (place >= step) & (i < line_ticks - 1))
        def _():
            fold(place - step, 0)

        @pl.when((k == 1) & (place + step < length) & (i < line_ticks - 1))
        def _():
            fold(place + step, 0)

        @pl.when(i == ticks - 2)
        def _():
            for j in range(n_row // 2):
                quarter = lax.rem(core_peer + 2 * j, n_row)

                def arrived(c, carry, quarter=quarter):
                    core_copy(quarter, c).wait_recv()
                    return carry

                lax.fori_loop(0, CHUNKS, arrived, 0)

            def early(origin, carry):
                @pl.when((origin - place < length - 1) & (place - origin < length - 1))
                def _():
                    fold(origin, 1)

                return carry

            lax.fori_loop(0, length, early, 0)

        return carry

    lax.fori_loop(0, ticks, tick, 0)
    lax.fori_loop(ticks, max(ticks, rows // tile), norm_tile, 0)

    @pl.when((place == 0) | (place == length - 1))
    def _():
        last = length - 1 - place
        fold(last, 0)
        fold(last, 1)

    logs = (high[...] + jnp.log2(total[...])) * LN2
    partials[my_row] = logs[0:2, :]
    outgoing[...] = logs[2:4, :]

    def row_copy(slot, peer):
        return pltpu.make_async_remote_copy(
            src_ref=partials.at[slot],
            dst_ref=partials.at[slot],
            send_sem=row_send.at[peer],
            recv_sem=part_recv.at[slot],
            device_id={"row": peer},
            device_id_type=MESH,
        )

    def side_copy(row, peer):
        return pltpu.make_async_remote_copy(
            src_ref=outgoing,
            dst_ref=partials.at[n_row + row],
            send_sem=side_send.at[peer],
            recv_sem=part_recv.at[n_row + row],
            device_id={"blk": other, "row": peer},
            device_id_type=MESH,
        )

    for peer in row_peers + [my_row]:
        side_copy(my_row, peer).start()
    for peer in row_peers:
        row_copy(my_row, peer).start()
    for peer in row_peers:
        row_copy(peer, peer).wait_recv()
    for peer in row_peers + [my_row]:
        side_copy(peer, peer).wait_recv()
    parts = [partials[i] for i in range(2 * n_row)]
    top = functools.reduce(jnp.maximum, parts)
    mass = functools.reduce(jnp.add, [jnp.exp(part - top) for part in parts])
    logs = top + jnp.log(mass) - pool_norms[...] * LN2
    ratio = logs[0:1, :] - logs[1:2, :]
    logs_out[...] = logs

    local_mean = jnp.sum(ratio, axis=1, keepdims=True) / rows
    local_spread = jnp.sum(jnp.square(ratio - local_mean), axis=1, keepdims=True)
    lanes = stats.shape[2]
    stats[me, 0:1, :] = jnp.broadcast_to(local_mean, (1, lanes))
    stats[me, 1:2, :] = jnp.broadcast_to(local_spread, (1, lanes))

    def stat_copy(slot, peer):
        return pltpu.make_async_remote_copy(
            src_ref=stats.at[slot],
            dst_ref=stats.at[slot],
            send_sem=stat_send.at[peer],
            recv_sem=stat_recv.at[slot],
            device_id={"blk": peer},
            device_id_type=MESH,
        )

    def stat_start(i, carry):
        stat_copy(me, lax.rem(me + i, n_blk)).start()
        return carry

    def stat_wait(i, carry):
        peer = lax.rem(me + i, n_blk)
        stat_copy(peer, peer).wait_recv()
        return carry

    lax.fori_loop(1, n_blk, stat_start, 0)

    for k in range(2):

        def sent(origin, carry, k=k):
            @pl.when((origin <= place) & (place < length - 1))
            def _():
                line_copy(origin, k, gathered.at[origin, k], 1, right_send).wait_send()

            @pl.when((origin >= place) & (place > 0))
            def _():
                line_copy(origin, k, gathered.at[origin, k], -1, left_send).wait_send()

            return carry

        lax.fori_loop(0, length, sent, 0)

    def pool_sent(c, carry):
        cross_copy(c).wait_send()
        core_copy(my_row, c).wait_send()
        for peer in x_peers:
            x_copy(c, peer).wait_send()
            core_copy(peer, c).wait_send()
        return carry

    lax.fori_loop(0, CHUNKS, pool_sent, 0)
    for peer in row_peers:
        row_copy(my_row, peer).wait_send()
    for peer in row_peers + [my_row]:
        side_copy(my_row, peer).wait_send()

    lax.fori_loop(1, n_blk, stat_wait, 0)
    means = stats[:, 0, :]
    spreads = stats[:, 1, :]
    mean = jnp.sum(means, axis=0, keepdims=True) / n_blk
    spread = jnp.sum(spreads, axis=0, keepdims=True)
    spread = spread + rows * jnp.sum(jnp.square(means - mean), axis=0, keepdims=True)
    scale = jnp.sqrt(spread / (rows * n_blk) + 1e-05)
    mean_out[...] = jnp.broadcast_to(mean[:, 0:1], mean_out.shape)
    scale_out[...] = jnp.broadcast_to(scale[:, 0:1], scale_out.shape)

    def stat_sent(i, carry):
        stat_copy(me, lax.rem(me + i, n_blk)).wait_send()
        return carry

    lax.fori_loop(1, n_blk, stat_sent, 0)


def body(n_blk, n_row, pool_embeds, target_samples, reference_samples):
    rows, depth = pool_embeds.shape
    width = target_samples.shape[0]
    length = n_blk // 2
    dma = pltpu.SemaphoreType.DMA
    flops = 2 * rows * depth * 2 * width * n_blk
    logs, mean, scale = pl.pallas_call(
        functools.partial(density_kernel, n_blk, n_row),
        out_shape=[
            jax.ShapeDtypeStruct((2, rows), jnp.float32),
            jax.ShapeDtypeStruct((1, rows), jnp.float32),
            jax.ShapeDtypeStruct((1, rows), jnp.float32),
        ],
        in_specs=[pl.BlockSpec(memory_space=pl.ANY)] * 3,
        out_specs=[pl.BlockSpec(memory_space=pltpu.VMEM)] * 3,
        scratch_shapes=[
            pltpu.VMEM((rows, depth), jnp.bfloat16),
            pltpu.VMEM((n_row, CHUNKS, rows // n_row // CHUNKS, depth), jnp.bfloat16),
            pltpu.VMEM((length, 2, width, depth), jnp.bfloat16),
            pltpu.VMEM((1, rows), jnp.float32),
            pltpu.VMEM((4, rows), jnp.float32),
            pltpu.VMEM((4, rows), jnp.float32),
            pltpu.VMEM((2 * n_row, 2, rows), jnp.float32),
            pltpu.VMEM((2, rows), jnp.float32),
            pltpu.VMEM((n_blk, 2, 128), jnp.float32),
            dma((3,)),
            dma((length, 2)),
            dma((length, 2)),
            dma((length, 2)),
            dma((CHUNKS,)),
            dma((n_row, CHUNKS)),
            dma((n_row, CHUNKS)),
            dma((n_row, CHUNKS)),
            dma((n_row,)),
            dma((n_row,)),
            dma((2 * n_row,)),
            dma((n_blk,)),
            dma((n_blk,)),
        ],
        compiler_params=pltpu.CompilerParams(
            collective_id=0, has_side_effects=True, vmem_limit_bytes=62 * 1024 * 1024
        ),
        cost_estimate=pl.CostEstimate(flops=flops, bytes_accessed=2 * rows * depth, transcendentals=0),
    )(pool_embeds, target_samples, reference_samples)
    ratio = logs[0] - logs[1]
    return ratio, (ratio - mean[0]) / scale[0]


def solution(mesh):
    in_specs = (P("blk", None), P(("blk", "row"), None), P(("blk", "row"), None))
    out_specs = (P("blk"), P("blk"))
    part = functools.partial(body, mesh.shape["blk"], mesh.shape["row"])
    return jax.shard_map(part, mesh=mesh, in_specs=in_specs, out_specs=out_specs, check_vma=False)
```

```python
import functools
import math

import jax
import jax.numpy as jnp
from jax import lax
from jax.experimental import pallas as pl
from jax.experimental.pallas import tpu as pltpu
from jax.sharding import PartitionSpec as P

KERNEL_GAIN = 30.0
LOG2E = math.log2(math.e)
LN2 = math.log(2.0)
CHUNKS = 4
MESH = pl.DeviceIdType.MESH


def density_kernel(
    n_blk,
    n_row,
    pool_hbm,
    target_hbm,
    ref_hbm,
    target_out,
    ref_out,
    mean_out,
    scale_out,
    pool,
    other_pool,
    gathered,
    pool_norms,
    high,
    total,
    partials,
    outgoing,
    stats,
    load_sem,
    right_send,
    left_send,
    line_recv,
    cross_send,
    x_send,
    core_send,
    pool_recv,
    row_send,
    side_send,
    part_recv,
    stat_send,
    stat_recv,
):
    me = lax.axis_index("blk")
    my_row = lax.axis_index("row")
    length = n_blk // 2
    place = me // 2
    other = me + 1 - 2 * lax.rem(me, 2)
    core = lax.rem(my_row, 2)
    core_peer = my_row + 1 - 2 * core
    x_peers = [lax.rem(my_row + 2 * j, n_row) for j in range(1, n_row // 2)]
    row_peers = [lax.rem(my_row + i, n_row) for i in range(1, n_row)]
    rows, depth = pool.shape
    width = target_hbm.shape[0]
    chunk = other_pool.shape[2]
    factor = KERNEL_GAIN / depth * LOG2E
    sources = (target_hbm, ref_hbm)
    nt = (((1,), (1,)), ((), ()))

    pool_load = pltpu.make_async_copy(pool_hbm, pool, load_sem.at[2])
    pool_load.start()
    own_loads = [
        pltpu.make_async_copy(sources[k], gathered.at[place, k], load_sem.at[k]) for k in range(2)
    ]
    for load in own_loads:
        load.start()

    barrier = pltpu.get_barrier_semaphore()

    near = pl.semaphore_signal

    @pl.when(place < length - 1)
    def _():
        near(barrier, inc=1, device_id={"blk": me + 2}, device_id_type=MESH)

    @pl.when(place > 0)
    def _():
        near(barrier, inc=1, device_id={"blk": me - 2}, device_id_type=MESH)

    near(barrier, inc=1, device_id={"blk": other}, device_id_type=MESH)
    for peer in x_peers + [core_peer]:
        near(barrier, inc=1, device_id={"row": peer}, device_id_type=MESH)
    ends = (place == 0).astype(jnp.int32) + (place == length - 1).astype(jnp.int32)
    pl.semaphore_wait(barrier, 4 + len(x_peers) - ends)

    def line_copy(origin, k, src, step, sems):
        return pltpu.make_async_remote_copy(
            src_ref=src,
            dst_ref=gathered.at[origin, k],
            send_sem=sems.at[origin, k],
            recv_sem=line_recv.at[origin, k],
            device_id={"blk": me + 2 * step},
            device_id_type=MESH,
        )

    def cross_copy(c):
        at = pl.multiple_of((my_row * CHUNKS + c) * chunk, chunk)
        return pltpu.make_async_remote_copy(
            src_ref=pool_hbm.at[pl.ds(at, chunk)],
            dst_ref=other_pool.at[my_row, c],
            send_sem=cross_send.at[c],
            recv_sem=pool_recv.at[my_row, c],
            device_id={"blk": other},
            device_id_type=MESH,
        )

    def row_relay(quarter, c, peer, send_sem):
        return pltpu.make_async_remote_copy(
            src_ref=other_pool.at[quarter, c],
            dst_ref=other_pool.at[quarter, c],
            send_sem=send_sem,
            recv_sem=pool_recv.at[quarter, c],
            device_id={"row": peer},
            device_id_type=MESH,
        )

    def core_copy(quarter, c):
        return row_relay(quarter, c, core_peer, core_send.at[quarter, c])

    def x_copy(c, peer):
        return row_relay(my_row, c, peer, x_send.at[peer, c])

    for k in range(2):

        @pl.when(place < length - 1)
        def _(k=k):
            line_copy(place, k, sources[k], 1, right_send).start()

        @pl.when(place > 0)
        def _(k=k):
            line_copy(place, k, sources[k], -1, left_send).start()

    for c in range(CHUNKS):
        cross_copy(c).start()

    high[...] = jnp.full_like(high, -1e30)
    total[...] = jnp.zeros_like(total)

    def fold(origin, which, count=1):
        block = gathered[pl.ds(origin, count)].reshape(count * 2 * width, depth)
        columns = pool[...] if which == 0 else other_pool[...].reshape(rows, depth)
        norms = jnp.sum(jnp.square(block.astype(jnp.float32)), axis=1, keepdims=True) * factor
        products = lax.dot_general(block, columns, nt, preferred_element_type=jnp.float32)
        scores_all = products * (2.0 * factor) - norms
        for k in range(2):
            pieces = [scores_all[(2 * j + k) * width : (2 * j + k + 1) * width, :] for j in range(count)]
            at = 2 * which + k
            old = high[at : at + 1, :]
            best = [jnp.max(piece, axis=0, keepdims=True) for piece in pieces]
            new = functools.reduce(jnp.maximum, best, old)
            sums = [jnp.sum(jnp.exp2(piece - new), axis=0, keepdims=True) for piece in pieces]
            total[at : at + 1, :] = total[at : at + 1, :] * jnp.exp2(old - new) + sum(sums)
            high[at : at + 1, :] = new

    pool_load.wait()
    for load in own_loads:
        load.wait()
    fold(place, 0)

    ones = jnp.ones((8, depth), jnp.bfloat16)
    tile = 256 if rows % 256 == 0 else rows

    def norm_tile(i, carry):
        at = pl.multiple_of(i * tile, tile)
        squares = jnp.square(pool[pl.ds(at, tile), :].astype(jnp.float32))
        coarse = squares.astype(jnp.bfloat16)
        fine = (squares - coarse.astype(jnp.float32)).astype(jnp.bfloat16)
        sums = lax.dot_general(ones, coarse, nt, preferred_element_type=jnp.float32)
        sums = sums + lax.dot_general(ones, fine, nt, preferred_element_type=jnp.float32)
        pool_norms[:, pl.ds(at, tile)] = sums[0:1, :] * factor
        return carry

    line_ticks = 2 * (length - 1)
    ticks = max(line_ticks, CHUNKS + 2)

    def tick(i, carry):
        step = i // 2 + 1
        k = lax.rem(i, 2)

        @pl.when((i < line_ticks) & (place >= step))
        def _():
            origin = place - step
            block = gathered.at[origin, k]
            line_copy(origin, k, block, 1, right_send).wait_recv()

            @pl.when(place < length - 1)
            def _():
                line_copy(origin, k, block, 1, right_send).start()

        @pl.when((i < line_ticks) & (place + step < length))
        def _():
            origin = place + step
            block = gathered.at[origin, k]
            line_copy(origin, k, block, -1, left_send).wait_recv()

            @pl.when(place > 0)
            def _():
                line_copy(origin, k, block, -1, left_send).start()

        @pl.when(i < CHUNKS)
        def _():
            cross_copy(i).wait_recv()
            for peer in x_peers:
                x_copy(i, peer).start()
            core_copy(my_row, i).start()

        @pl.when((i >= 1) & (i <= CHUNKS))
        def _():
            for peer in x_peers:
                row_relay(peer, i - 1, peer, x_send.at[peer, i - 1]).wait_recv()
                core_copy(peer, i - 1).start()

        @pl.when(i < rows // tile)
        def _():
            norm_tile(i, 0)

        @pl.when((k == 1) & (place >= step) & (i < line_ticks - 1))
        def _():
            fold(place - step, 0)

        @pl.when((k == 1) & (place + step < length) & (i < line_ticks - 1))
        def _():
            fold(place + step, 0)

        @pl.when(i == ticks - 2)
        def _():
            for j in range(n_row // 2):
                quarter = lax.rem(core_peer + 2 * j, n_row)

                def arrived(c, carry, quarter=quarter):
                    core_copy(quarter, c).wait_recv()
                    return carry

                lax.fori_loop(0, CHUNKS, arrived, 0)

            first = jnp.minimum(place, 1)
            if length <= 4:
                fold(first, 1, length - 1)
            else:

                def early(origin, carry):
                    fold(origin, 1)
                    return carry

                lax.fori_loop(first, first + length - 1, early, 0)

            @pl.when((place > 0) & (place < length - 1))
            def _():
                fold(0, 1)

        return carry

    lax.fori_loop(0, ticks, tick, 0)
    lax.fori_loop(ticks, max(ticks, rows // tile), norm_tile, 0)

    @pl.when((place == 0) | (place == length - 1))
    def _():
        last = length - 1 - place
        fold(last, 0)
        fold(last, 1)

    logs = (high[...] + jnp.log2(total[...])) * LN2
    partials[my_row] = logs[0:2, :]
    outgoing[...] = logs[2:4, :]

    def row_copy(slot, peer):
        return pltpu.make_async_remote_copy(
            src_ref=partials.at[slot],
            dst_ref=partials.at[slot],
            send_sem=row_send.at[peer],
            recv_sem=part_recv.at[slot],
            device_id={"row": peer},
            device_id_type=MESH,
        )

    def side_copy(row, peer):
        return pltpu.make_async_remote_copy(
            src_ref=outgoing,
            dst_ref=partials.at[n_row + row],
            send_sem=side_send.at[peer],
            recv_sem=part_recv.at[n_row + row],
            device_id={"blk": other, "row": peer},
            device_id_type=MESH,
        )

    for peer in row_peers + [my_row]:
        side_copy(my_row, peer).start()
    for peer in row_peers:
        row_copy(my_row, peer).start()
    for peer in row_peers:
        row_copy(peer, peer).wait_recv()
    for peer in row_peers + [my_row]:
        side_copy(peer, peer).wait_recv()
    parts = [partials[i] for i in range(2 * n_row)]
    top = functools.reduce(jnp.maximum, parts)
    mass = functools.reduce(jnp.add, [jnp.exp(part - top) for part in parts])
    logs = top + jnp.log(mass) - pool_norms[...] * LN2
    ratio = logs[0:1, :] - logs[1:2, :]
    target_out[...] = logs[0:1, :]
    ref_out[...] = logs[1:2, :]

    local_mean = jnp.sum(ratio, axis=1, keepdims=True) / rows
    local_spread = jnp.sum(jnp.square(ratio - local_mean), axis=1, keepdims=True)
    lanes = stats.shape[2]
    stats[me, 0:1, :] = jnp.broadcast_to(local_mean, (1, lanes))
    stats[me, 1:2, :] = jnp.broadcast_to(local_spread, (1, lanes))

    def stat_copy(slot, peer):
        return pltpu.make_async_remote_copy(
            src_ref=stats.at[slot],
            dst_ref=stats.at[slot],
            send_sem=stat_send.at[peer],
            recv_sem=stat_recv.at[slot],
            device_id={"blk": peer},
            device_id_type=MESH,
        )

    def stat_start(i, carry):
        stat_copy(me, lax.rem(me + i, n_blk)).start()
        return carry

    def stat_wait(i, carry):
        peer = lax.rem(me + i, n_blk)
        stat_copy(peer, peer).wait_recv()
        return carry

    lax.fori_loop(1, n_blk, stat_start, 0)

    for k in range(2):

        def sent(origin, carry, k=k):
            @pl.when((origin <= place) & (place < length - 1))
            def _():
                line_copy(origin, k, gathered.at[origin, k], 1, right_send).wait_send()

            @pl.when((origin >= place) & (place > 0))
            def _():
                line_copy(origin, k, gathered.at[origin, k], -1, left_send).wait_send()

            return carry

        lax.fori_loop(0, length, sent, 0)

    def pool_sent(c, carry):
        cross_copy(c).wait_send()
        core_copy(my_row, c).wait_send()
        for peer in x_peers:
            x_copy(c, peer).wait_send()
            core_copy(peer, c).wait_send()
        return carry

    lax.fori_loop(0, CHUNKS, pool_sent, 0)
    for peer in row_peers:
        row_copy(my_row, peer).wait_send()
    for peer in row_peers + [my_row]:
        side_copy(my_row, peer).wait_send()

    lax.fori_loop(1, n_blk, stat_wait, 0)
    means = stats[:, 0, :]
    spreads = stats[:, 1, :]
    mean = jnp.sum(means, axis=0, keepdims=True) / n_blk
    spread = jnp.sum(spreads, axis=0, keepdims=True)
    spread = spread + rows * jnp.sum(jnp.square(means - mean), axis=0, keepdims=True)
    scale = jnp.sqrt(spread / (rows * n_blk) + 1e-05)
    mean_out[...] = jnp.broadcast_to(mean[:, 0:1], mean_out.shape)
    scale_out[...] = jnp.broadcast_to(scale[:, 0:1], scale_out.shape)

    def stat_sent(i, carry):
        stat_copy(me, lax.rem(me + i, n_blk)).wait_send()
        return carry

    lax.fori_loop(1, n_blk, stat_sent, 0)


def body(n_blk, n_row, pool_embeds, target_samples, reference_samples):
    rows, depth = pool_embeds.shape
    width = target_samples.shape[0]
    length = n_blk // 2
    dma = pltpu.SemaphoreType.DMA
    flops = 2 * rows * depth * 2 * width * n_blk
    log_target, log_ref, mean, scale = pl.pallas_call(
        functools.partial(density_kernel, n_blk, n_row),
        out_shape=[
            pltpu.VMEM((1, rows), jnp.float32),
            pltpu.VMEM((1, rows), jnp.float32),
            pltpu.VMEM((1, rows), jnp.float32),
            pltpu.VMEM((1, rows), jnp.float32),
        ],
        in_specs=[pl.BlockSpec(memory_space=pltpu.HBM)] * 3,
        out_specs=[pl.BlockSpec(memory_space=pltpu.VMEM)] * 4,
        scratch_shapes=[
            pltpu.VMEM((rows, depth), jnp.bfloat16),
            pltpu.VMEM((n_row, CHUNKS, rows // n_row // CHUNKS, depth), jnp.bfloat16),
            pltpu.VMEM((length, 2, width, depth), jnp.bfloat16),
            pltpu.VMEM((1, rows), jnp.float32),
            pltpu.VMEM((4, rows), jnp.float32),
            pltpu.VMEM((4, rows), jnp.float32),
            pltpu.VMEM((2 * n_row, 2, rows), jnp.float32),
            pltpu.VMEM((2, rows), jnp.float32),
            pltpu.VMEM((n_blk, 2, 128), jnp.float32),
            dma((3,)),
            dma((length, 2)),
            dma((length, 2)),
            dma((length, 2)),
            dma((CHUNKS,)),
            dma((n_row, CHUNKS)),
            dma((n_row, CHUNKS)),
            dma((n_row, CHUNKS)),
            dma((n_row,)),
            dma((n_row,)),
            dma((2 * n_row,)),
            dma((n_blk,)),
            dma((n_blk,)),
        ],
        compiler_params=pltpu.CompilerParams(
            collective_id=0, has_side_effects=True, vmem_limit_bytes=62 * 1024 * 1024
        ),
        cost_estimate=pl.CostEstimate(flops=flops, bytes_accessed=2 * rows * depth, transcendentals=0),
    )(pool_embeds, target_samples, reference_samples)
    ratio = log_target.reshape(rows) - log_ref.reshape(rows)
    return ratio, (ratio - mean.reshape(rows)) / scale.reshape(rows)


def solution(mesh):
    in_specs = (P("blk", None), P(("blk", "row"), None), P(("blk", "row"), None))
    out_specs = (P("blk"), P("blk"))
    part = functools.partial(body, mesh.shape["blk"], mesh.shape["row"])
    return jax.shard_map(part, mesh=mesh, in_specs=in_specs, out_specs=out_specs, check_vma=False)
```

```python
import functools
import math

import jax
import jax.numpy as jnp
from jax import lax
from jax.experimental import pallas as pl
from jax.experimental.pallas import tpu as pltpu
from jax.sharding import PartitionSpec as P

KERNEL_GAIN = 30.0
LOG2E = math.log2(math.e)
LN2 = math.log(2.0)
CHUNKS = 8
GROUPS = 4
MESH = pl.DeviceIdType.MESH


def density_kernel(
    n_blk,
    n_row,
    pool_hbm,
    target_hbm,
    ref_hbm,
    target_out,
    ref_out,
    mean_out,
    scale_out,
    pool,
    other_pool,
    gathered,
    pool_norms,
    high,
    total,
    partials,
    outgoing,
    stats,
    load_sem,
    right_send,
    left_send,
    line_recv,
    cross_send,
    x_send,
    core_send,
    pool_recv,
    row_send,
    side_send,
    part_recv,
    stat_send,
    stat_recv,
):
    me = lax.axis_index("blk")
    my_row = lax.axis_index("row")
    length = n_blk // 2
    place = me // 2
    other = me + 1 - 2 * lax.rem(me, 2)
    core = lax.rem(my_row, 2)
    core_peer = my_row + 1 - 2 * core
    x_peers = [lax.rem(my_row + 2 * j, n_row) for j in range(1, n_row // 2)]
    row_peers = [lax.rem(my_row + i, n_row) for i in range(1, n_row)]
    rows, depth = pool.shape
    width = target_hbm.shape[0]
    chunk = other_pool.shape[2]
    group = rows // GROUPS
    per_group = CHUNKS // GROUPS
    factor = KERNEL_GAIN / depth * LOG2E
    sources = (target_hbm, ref_hbm)
    nt = (((1,), (1,)), ((), ()))

    pool_load = pltpu.make_async_copy(pool_hbm, pool, load_sem.at[2])
    pool_load.start()
    own_loads = [
        pltpu.make_async_copy(sources[k], gathered.at[place, k], load_sem.at[k]) for k in range(2)
    ]
    for load in own_loads:
        load.start()

    barrier = pltpu.get_barrier_semaphore()

    near = pl.semaphore_signal

    @pl.when(place < length - 1)
    def _():
        near(barrier, inc=1, device_id={"blk": me + 2}, device_id_type=MESH)

    @pl.when(place > 0)
    def _():
        near(barrier, inc=1, device_id={"blk": me - 2}, device_id_type=MESH)

    near(barrier, inc=1, device_id={"blk": other}, device_id_type=MESH)
    for peer in x_peers + [core_peer]:
        near(barrier, inc=1, device_id={"row": peer}, device_id_type=MESH)
    ends = (place == 0).astype(jnp.int32) + (place == length - 1).astype(jnp.int32)
    pl.semaphore_wait(barrier, 4 + len(x_peers) - ends)

    def line_copy(origin, k, src, step, sems):
        return pltpu.make_async_remote_copy(
            src_ref=src,
            dst_ref=gathered.at[origin, k],
            send_sem=sems.at[origin, k],
            recv_sem=line_recv.at[origin, k],
            device_id={"blk": me + 2 * step},
            device_id_type=MESH,
        )

    def cross_copy(c):
        at = pl.multiple_of((c * n_row + my_row) * chunk, chunk)
        return pltpu.make_async_remote_copy(
            src_ref=pool_hbm.at[pl.ds(at, chunk)],
            dst_ref=other_pool.at[c, my_row],
            send_sem=cross_send.at[c],
            recv_sem=pool_recv.at[my_row, c],
            device_id={"blk": other},
            device_id_type=MESH,
        )

    def row_relay(quarter, c, peer, send_sem):
        return pltpu.make_async_remote_copy(
            src_ref=other_pool.at[c, quarter],
            dst_ref=other_pool.at[c, quarter],
            send_sem=send_sem,
            recv_sem=pool_recv.at[quarter, c],
            device_id={"row": peer},
            device_id_type=MESH,
        )

    def core_copy(quarter, c):
        return row_relay(quarter, c, core_peer, core_send.at[quarter, c])

    def x_copy(c, peer):
        return row_relay(my_row, c, peer, x_send.at[peer, c])

    for k in range(2):

        @pl.when(place < length - 1)
        def _(k=k):
            line_copy(place, k, sources[k], 1, right_send).start()

        @pl.when(place > 0)
        def _(k=k):
            line_copy(place, k, sources[k], -1, left_send).start()

    for c in range(CHUNKS):
        cross_copy(c).start()

    high[...] = jnp.full_like(high, -1e30)
    total[...] = jnp.zeros_like(total)

    def fold(origin, which, count=1, part=None):
        block = gathered[pl.ds(origin, count)].reshape(count * 2 * width, depth)
        if which == 0:
            columns = pool[...]
        elif part is None:
            columns = other_pool[...].reshape(rows, depth)
        else:
            columns = other_pool[part * per_group : (part + 1) * per_group].reshape(group, depth)
        across = slice(0, rows) if part is None else slice(part * group, (part + 1) * group)
        norms = jnp.sum(jnp.square(block.astype(jnp.float32)), axis=1, keepdims=True) * factor
        products = lax.dot_general(block, columns, nt, preferred_element_type=jnp.float32)
        scores_all = products * (2.0 * factor) - norms
        for k in range(2):
            pieces = [scores_all[(2 * j + k) * width : (2 * j + k + 1) * width, :] for j in range(count)]
            at = 2 * which + k
            old = high[at : at + 1, across]
            best = [jnp.max(piece, axis=0, keepdims=True) for piece in pieces]
            new = functools.reduce(jnp.maximum, best, old)
            sums = [jnp.sum(jnp.exp2(piece - new), axis=0, keepdims=True) for piece in pieces]
            total[at : at + 1, across] = total[at : at + 1, across] * jnp.exp2(old - new) + sum(sums)
            high[at : at + 1, across] = new

    pool_load.wait()
    for load in own_loads:
        load.wait()
    fold(place, 0)

    ones = jnp.ones((8, depth), jnp.bfloat16)
    tile = 256 if rows % 256 == 0 else rows

    def norm_tile(i, carry):
        at = pl.multiple_of(i * tile, tile)
        squares = jnp.square(pool[pl.ds(at, tile), :].astype(jnp.float32))
        coarse = squares.astype(jnp.bfloat16)
        fine = (squares - coarse.astype(jnp.float32)).astype(jnp.bfloat16)
        sums = lax.dot_general(ones, coarse, nt, preferred_element_type=jnp.float32)
        sums = sums + lax.dot_general(ones, fine, nt, preferred_element_type=jnp.float32)
        pool_norms[:, pl.ds(at, tile)] = sums[0:1, :] * factor
        return carry

    line_ticks = 2 * (length - 1)
    ticks = max(line_ticks, CHUNKS // 2 + 2)

    def from_side(c):
        @pl.when(c < CHUNKS)
        def _():
            cross_copy(c).wait_recv()
            for peer in x_peers:
                x_copy(c, peer).start()
            core_copy(my_row, c).start()

    def from_x(c):
        @pl.when((c >= 0) & (c < CHUNKS))
        def _():
            for peer in x_peers:
                row_relay(peer, c, peer, x_send.at[peer, c]).wait_recv()
                core_copy(peer, c).start()

    def fold_other(part):
        for j in range(n_row // 2):
            quarter = lax.rem(core_peer + 2 * j, n_row)
            for c in range(part * per_group, (part + 1) * per_group):
                core_copy(quarter, c).wait_recv()
        first = jnp.minimum(place, 1)
        if length <= 4:
            fold(first, 1, length - 1, part)
        else:

            def early(origin, carry):
                fold(origin, 1, 1, part)
                return carry

            lax.fori_loop(first, first + length - 1, early, 0)

        @pl.when((place > 0) & (place < length - 1))
        def _():
            fold(0, 1, 1, part)

    def tick(i, carry):
        step = i // 2 + 1
        k = lax.rem(i, 2)
        from_side(2 * i)

        @pl.when((i < line_ticks) & (place >= step))
        def _():
            origin = place - step
            block = gathered.at[origin, k]
            line_copy(origin, k, block, 1, right_send).wait_recv()

            @pl.when(place < length - 1)
            def _():
                line_copy(origin, k, block, 1, right_send).start()

        @pl.when((i < line_ticks) & (place + step < length))
        def _():
            origin = place + step
            block = gathered.at[origin, k]
            line_copy(origin, k, block, -1, left_send).wait_recv()

            @pl.when(place > 0)
            def _():
                line_copy(origin, k, block, -1, left_send).start()

        from_x(2 * i - 1)
        from_side(2 * i + 1)
        from_x(2 * i)

        @pl.when(i < rows // tile)
        def _():
            norm_tile(i, 0)

        @pl.when((k == 1) & (place >= step) & (i < line_ticks - 1))
        def _():
            fold(place - step, 0)

        @pl.when((k == 1) & (place + step < length) & (i < line_ticks - 1))
        def _():
            fold(place + step, 0)

        @pl.when(i == ticks - 3)
        def _():
            for part in range(GROUPS // 2):
                fold_other(part)

        @pl.when(i == ticks - 2)
        def _():
            for part in range(GROUPS // 2, GROUPS):
                fold_other(part)

        return carry

    lax.fori_loop(0, ticks, tick, 0)
    lax.fori_loop(ticks, max(ticks, rows // tile), norm_tile, 0)

    @pl.when((place == 0) | (place == length - 1))
    def _():
        last = length - 1 - place
        fold(last, 0)
        fold(last, 1)

    logs = (high[...] + jnp.log2(total[...])) * LN2
    partials[my_row] = logs[0:2, :]
    outgoing[...] = logs[2:4, :]

    def row_copy(slot, peer):
        return pltpu.make_async_remote_copy(
            src_ref=partials.at[slot],
            dst_ref=partials.at[slot],
            send_sem=row_send.at[peer],
            recv_sem=part_recv.at[slot],
            device_id={"row": peer},
            device_id_type=MESH,
        )

    def side_copy(row, peer):
        return pltpu.make_async_remote_copy(
            src_ref=outgoing,
            dst_ref=partials.at[n_row + row],
            send_sem=side_send.at[peer],
            recv_sem=part_recv.at[n_row + row],
            device_id={"blk": other, "row": peer},
            device_id_type=MESH,
        )

    for peer in row_peers + [my_row]:
        side_copy(my_row, peer).start()
    for peer in row_peers:
        row_copy(my_row, peer).start()
    for peer in row_peers:
        row_copy(peer, peer).wait_recv()
    for peer in row_peers + [my_row]:
        side_copy(peer, peer).wait_recv()
    parts = [partials[i] for i in range(2 * n_row)]
    top = functools.reduce(jnp.maximum, parts)
    mass = functools.reduce(jnp.add, [jnp.exp(part - top) for part in parts])
    logs = top + jnp.log(mass) - pool_norms[...] * LN2
    ratio = logs[0:1, :] - logs[1:2, :]
    target_out[...] = logs[0:1, :]
    ref_out[...] = logs[1:2, :]

    local_mean = jnp.sum(ratio, axis=1, keepdims=True) / rows
    local_spread = jnp.sum(jnp.square(ratio - local_mean), axis=1, keepdims=True)
    lanes = stats.shape[2]
    stats[me, 0:1, :] = jnp.broadcast_to(local_mean, (1, lanes))
    stats[me, 1:2, :] = jnp.broadcast_to(local_spread, (1, lanes))

    def stat_copy(slot, peer):
        return pltpu.make_async_remote_copy(
            src_ref=stats.at[slot],
            dst_ref=stats.at[slot],
            send_sem=stat_send.at[peer],
            recv_sem=stat_recv.at[slot],
            device_id={"blk": peer},
            device_id_type=MESH,
        )

    def stat_start(i, carry):
        stat_copy(me, lax.rem(me + i, n_blk)).start()
        return carry

    def stat_wait(i, carry):
        peer = lax.rem(me + i, n_blk)
        stat_copy(peer, peer).wait_recv()
        return carry

    lax.fori_loop(1, n_blk, stat_start, 0)

    for k in range(2):

        def sent(origin, carry, k=k):
            @pl.when((origin <= place) & (place < length - 1))
            def _():
                line_copy(origin, k, gathered.at[origin, k], 1, right_send).wait_send()

            @pl.when((origin >= place) & (place > 0))
            def _():
                line_copy(origin, k, gathered.at[origin, k], -1, left_send).wait_send()

            return carry

        lax.fori_loop(0, length, sent, 0)

    def pool_sent(c, carry):
        cross_copy(c).wait_send()
        core_copy(my_row, c).wait_send()
        for peer in x_peers:
            x_copy(c, peer).wait_send()
            core_copy(peer, c).wait_send()
        return carry

    lax.fori_loop(0, CHUNKS, pool_sent, 0)
    for peer in row_peers:
        row_copy(my_row, peer).wait_send()
    for peer in row_peers + [my_row]:
        side_copy(my_row, peer).wait_send()

    lax.fori_loop(1, n_blk, stat_wait, 0)
    means = stats[:, 0, :]
    spreads = stats[:, 1, :]
    mean = jnp.sum(means, axis=0, keepdims=True) / n_blk
    spread = jnp.sum(spreads, axis=0, keepdims=True)
    spread = spread + rows * jnp.sum(jnp.square(means - mean), axis=0, keepdims=True)
    scale = jnp.sqrt(spread / (rows * n_blk) + 1e-05)
    mean_out[...] = jnp.broadcast_to(mean[:, 0:1], mean_out.shape)
    scale_out[...] = jnp.broadcast_to(scale[:, 0:1], scale_out.shape)

    def stat_sent(i, carry):
        stat_copy(me, lax.rem(me + i, n_blk)).wait_send()
        return carry

    lax.fori_loop(1, n_blk, stat_sent, 0)


def body(n_blk, n_row, pool_embeds, target_samples, reference_samples):
    rows, depth = pool_embeds.shape
    width = target_samples.shape[0]
    length = n_blk // 2
    dma = pltpu.SemaphoreType.DMA
    flops = 2 * rows * depth * 2 * width * n_blk
    log_target, log_ref, mean, scale = pl.pallas_call(
        functools.partial(density_kernel, n_blk, n_row),
        out_shape=[
            pltpu.VMEM((1, rows), jnp.float32),
            pltpu.VMEM((1, rows), jnp.float32),
            pltpu.VMEM((1, rows), jnp.float32),
            pltpu.VMEM((1, rows), jnp.float32),
        ],
        in_specs=[pl.BlockSpec(memory_space=pltpu.HBM)] * 3,
        out_specs=[pl.BlockSpec(memory_space=pltpu.VMEM)] * 4,
        scratch_shapes=[
            pltpu.VMEM((rows, depth), jnp.bfloat16),
            pltpu.VMEM((CHUNKS, n_row, rows // n_row // CHUNKS, depth), jnp.bfloat16),
            pltpu.VMEM((length, 2, width, depth), jnp.bfloat16),
            pltpu.VMEM((1, rows), jnp.float32),
            pltpu.VMEM((4, rows), jnp.float32),
            pltpu.VMEM((4, rows), jnp.float32),
            pltpu.VMEM((2 * n_row, 2, rows), jnp.float32),
            pltpu.VMEM((2, rows), jnp.float32),
            pltpu.VMEM((n_blk, 2, 128), jnp.float32),
            dma((3,)),
            dma((length, 2)),
            dma((length, 2)),
            dma((length, 2)),
            dma((CHUNKS,)),
            dma((n_row, CHUNKS)),
            dma((n_row, CHUNKS)),
            dma((n_row, CHUNKS)),
            dma((n_row,)),
            dma((n_row,)),
            dma((2 * n_row,)),
            dma((n_blk,)),
            dma((n_blk,)),
        ],
        compiler_params=pltpu.CompilerParams(
            collective_id=0, has_side_effects=True, vmem_limit_bytes=62 * 1024 * 1024
        ),
        cost_estimate=pl.CostEstimate(flops=flops, bytes_accessed=2 * rows * depth, transcendentals=0),
    )(pool_embeds, target_samples, reference_samples)
    ratio = log_target.reshape(rows) - log_ref.reshape(rows)
    return ratio, (ratio - mean.reshape(rows)) / scale.reshape(rows)


def solution(mesh):
    in_specs = (P("blk", None), P(("blk", "row"), None), P(("blk", "row"), None))
    out_specs = (P("blk"), P("blk"))
    part = functools.partial(body, mesh.shape["blk"], mesh.shape["row"])
    return jax.shard_map(part, mesh=mesh, in_specs=in_specs, out_specs=out_specs, check_vma=False)
```

```python
import functools
import math

import jax
import jax.numpy as jnp
from jax import lax
from jax.experimental import pallas as pl
from jax.experimental.pallas import tpu as pltpu
from jax.sharding import PartitionSpec as P

KERNEL_GAIN = 30.0
LOG2E = math.log2(math.e)
LN2 = math.log(2.0)
CHUNKS = 2
MESH = pl.DeviceIdType.MESH


def density_kernel(
    n_blk,
    n_row,
    pool_hbm,
    target_hbm,
    ref_hbm,
    target_out,
    ref_out,
    mean_out,
    scale_out,
    pool,
    other_pool,
    gathered,
    pool_norms,
    high,
    total,
    partials,
    outgoing,
    stats,
    load_sem,
    right_send,
    left_send,
    line_recv,
    cross_send,
    x_send,
    core_send,
    pool_recv,
    row_send,
    side_send,
    part_recv,
    stat_send,
    stat_recv,
):
    me = lax.axis_index("blk")
    my_row = lax.axis_index("row")
    length = n_blk // 2
    place = me // 2
    other = me + 1 - 2 * lax.rem(me, 2)
    core = lax.rem(my_row, 2)
    core_peer = my_row + 1 - 2 * core
    x_peers = [lax.rem(my_row + 2 * j, n_row) for j in range(1, n_row // 2)]
    row_peers = [lax.rem(my_row + i, n_row) for i in range(1, n_row)]
    rows, depth = pool.shape
    width = target_hbm.shape[0]
    chunk = other_pool.shape[2]
    factor = KERNEL_GAIN / depth * LOG2E
    sources = (target_hbm, ref_hbm)
    nt = (((1,), (1,)), ((), ()))

    pool_load = pltpu.make_async_copy(pool_hbm, pool, load_sem.at[2])
    pool_load.start()
    own_loads = [
        pltpu.make_async_copy(sources[k], gathered.at[place, k], load_sem.at[k]) for k in range(2)
    ]
    for load in own_loads:
        load.start()

    barrier = pltpu.get_barrier_semaphore()

    near = pl.semaphore_signal

    @pl.when(place < length - 1)
    def _():
        near(barrier, inc=1, device_id={"blk": me + 2}, device_id_type=MESH)

    @pl.when(place > 0)
    def _():
        near(barrier, inc=1, device_id={"blk": me - 2}, device_id_type=MESH)

    near(barrier, inc=1, device_id={"blk": other}, device_id_type=MESH)
    for peer in x_peers + [core_peer]:
        near(barrier, inc=1, device_id={"row": peer}, device_id_type=MESH)
    ends = (place == 0).astype(jnp.int32) + (place == length - 1).astype(jnp.int32)
    pl.semaphore_wait(barrier, 4 + len(x_peers) - ends)

    def line_copy(origin, k, src, step, sems):
        return pltpu.make_async_remote_copy(
            src_ref=src,
            dst_ref=gathered.at[origin, k],
            send_sem=sems.at[origin, k],
            recv_sem=line_recv.at[origin, k],
            device_id={"blk": me + 2 * step},
            device_id_type=MESH,
        )

    def cross_copy(c):
        at = pl.multiple_of((my_row * CHUNKS + c) * chunk, chunk)
        return pltpu.make_async_remote_copy(
            src_ref=pool_hbm.at[pl.ds(at, chunk)],
            dst_ref=other_pool.at[my_row, c],
            send_sem=cross_send.at[c],
            recv_sem=pool_recv.at[my_row, c],
            device_id={"blk": other},
            device_id_type=MESH,
        )

    def row_relay(quarter, c, peer, send_sem):
        return pltpu.make_async_remote_copy(
            src_ref=other_pool.at[quarter, c],
            dst_ref=other_pool.at[quarter, c],
            send_sem=send_sem,
            recv_sem=pool_recv.at[quarter, c],
            device_id={"row": peer},
            device_id_type=MESH,
        )

    def core_copy(quarter, c):
        return row_relay(quarter, c, core_peer, core_send.at[quarter, c])

    def x_copy(c, peer):
        return row_relay(my_row, c, peer, x_send.at[peer, c])

    for k in range(2):

        @pl.when(place < length - 1)
        def _(k=k):
            line_copy(place, k, sources[k], 1, right_send).start()

        @pl.when(place > 0)
        def _(k=k):
            line_copy(place, k, sources[k], -1, left_send).start()

    for c in range(CHUNKS):
        cross_copy(c).start()

    high[...] = jnp.full_like(high, -1e30)
    total[...] = jnp.zeros_like(total)

    def fold(origin, which, count=1):
        block = gathered[pl.ds(origin, count)].reshape(count * 2 * width, depth)
        columns = pool[...] if which == 0 else other_pool[...].reshape(rows, depth)
        norms = jnp.sum(jnp.square(block.astype(jnp.float32)), axis=1, keepdims=True) * factor
        products = lax.dot_general(block, columns, nt, preferred_element_type=jnp.float32)
        scores_all = products * (2.0 * factor) - norms
        for k in range(2):
            pieces = [scores_all[(2 * j + k) * width : (2 * j + k + 1) * width, :] for j in range(count)]
            at = 2 * which + k
            old = high[at : at + 1, :]
            best = [jnp.max(piece, axis=0, keepdims=True) for piece in pieces]
            new = functools.reduce(jnp.maximum, best, old)
            sums = [jnp.sum(jnp.exp2(piece - new), axis=0, keepdims=True) for piece in pieces]
            total[at : at + 1, :] = total[at : at + 1, :] * jnp.exp2(old - new) + sum(sums)
            high[at : at + 1, :] = new

    pool_load.wait()
    for load in own_loads:
        load.wait()
    fold(place, 0)

    ones = jnp.ones((8, depth), jnp.bfloat16)
    tile = 256 if rows % 256 == 0 else rows

    def norm_tile(i, carry):
        at = pl.multiple_of(i * tile, tile)
        squares = jnp.square(pool[pl.ds(at, tile), :].astype(jnp.float32))
        coarse = squares.astype(jnp.bfloat16)
        fine = (squares - coarse.astype(jnp.float32)).astype(jnp.bfloat16)
        sums = lax.dot_general(ones, coarse, nt, preferred_element_type=jnp.float32)
        sums = sums + lax.dot_general(ones, fine, nt, preferred_element_type=jnp.float32)
        pool_norms[:, pl.ds(at, tile)] = sums[0:1, :] * factor
        return carry

    line_ticks = 2 * (length - 1)
    ticks = max(line_ticks, CHUNKS + 2)

    def tick(i, carry):
        step = i // 2 + 1
        k = lax.rem(i, 2)

        @pl.when((i < line_ticks) & (place >= step))
        def _():
            origin = place - step
            block = gathered.at[origin, k]
            line_copy(origin, k, block, 1, right_send).wait_recv()

            @pl.when(place < length - 1)
            def _():
                line_copy(origin, k, block, 1, right_send).start()

        @pl.when((i < line_ticks) & (place + step < length))
        def _():
            origin = place + step
            block = gathered.at[origin, k]
            line_copy(origin, k, block, -1, left_send).wait_recv()

            @pl.when(place > 0)
            def _():
                line_copy(origin, k, block, -1, left_send).start()

        @pl.when(i < CHUNKS)
        def _():
            cross_copy(i).wait_recv()
            for peer in x_peers:
                x_copy(i, peer).start()
            core_copy(my_row, i).start()

        @pl.when((i >= 1) & (i <= CHUNKS))
        def _():
            for peer in x_peers:
                row_relay(peer, i - 1, peer, x_send.at[peer, i - 1]).wait_recv()
                core_copy(peer, i - 1).start()

        @pl.when(i < rows // tile)
        def _():
            norm_tile(i, 0)

        @pl.when((k == 1) & (place >= step) & (i < line_ticks - 1))
        def _():
            fold(place - step, 0)

        @pl.when((k == 1) & (place + step < length) & (i < line_ticks - 1))
        def _():
            fold(place + step, 0)

        @pl.when(i == ticks - 2)
        def _():
            for j in range(n_row // 2):
                quarter = lax.rem(core_peer + 2 * j, n_row)

                def arrived(c, carry, quarter=quarter):
                    core_copy(quarter, c).wait_recv()
                    return carry

                lax.fori_loop(0, CHUNKS, arrived, 0)

            first = jnp.minimum(place, 1)
            if length <= 4:
                fold(first, 1, length - 1)
            else:

                def early(origin, carry):
                    fold(origin, 1)
                    return carry

                lax.fori_loop(first, first + length - 1, early, 0)

            @pl.when((place > 0) & (place < length - 1))
            def _():
                fold(0, 1)

        return carry

    lax.fori_loop(0, ticks, tick, 0)
    lax.fori_loop(ticks, max(ticks, rows // tile), norm_tile, 0)

    @pl.when((place == 0) | (place == length - 1))
    def _():
        last = length - 1 - place
        fold(last, 0)
        fold(last, 1)

    logs = (high[...] + jnp.log2(total[...])) * LN2
    partials[my_row] = logs[0:2, :]
    outgoing[...] = logs[2:4, :]

    def row_copy(slot, peer):
        return pltpu.make_async_remote_copy(
            src_ref=partials.at[slot],
            dst_ref=partials.at[slot],
            send_sem=row_send.at[peer],
            recv_sem=part_recv.at[slot],
            device_id={"row": peer},
            device_id_type=MESH,
        )

    def side_copy(row, peer):
        return pltpu.make_async_remote_copy(
            src_ref=outgoing,
            dst_ref=partials.at[n_row + row],
            send_sem=side_send.at[peer],
            recv_sem=part_recv.at[n_row + row],
            device_id={"blk": other, "row": peer},
            device_id_type=MESH,
        )

    for peer in row_peers + [my_row]:
        side_copy(my_row, peer).start()
    for peer in row_peers:
        row_copy(my_row, peer).start()
    for peer in row_peers:
        row_copy(peer, peer).wait_recv()
    for peer in row_peers + [my_row]:
        side_copy(peer, peer).wait_recv()
    parts = [partials[i] for i in range(2 * n_row)]
    top = functools.reduce(jnp.maximum, parts)
    mass = functools.reduce(jnp.add, [jnp.exp(part - top) for part in parts])
    logs = top + jnp.log(mass) - pool_norms[...] * LN2
    ratio = logs[0:1, :] - logs[1:2, :]
    target_out[...] = logs[0:1, :]
    ref_out[...] = logs[1:2, :]

    local_mean = jnp.sum(ratio, axis=1, keepdims=True) / rows
    local_spread = jnp.sum(jnp.square(ratio - local_mean), axis=1, keepdims=True)
    lanes = stats.shape[2]
    stats[me, 0:1, :] = jnp.broadcast_to(local_mean, (1, lanes))
    stats[me, 1:2, :] = jnp.broadcast_to(local_spread, (1, lanes))

    def stat_copy(slot, peer):
        return pltpu.make_async_remote_copy(
            src_ref=stats.at[slot],
            dst_ref=stats.at[slot],
            send_sem=stat_send.at[peer],
            recv_sem=stat_recv.at[slot],
            device_id={"blk": peer},
            device_id_type=MESH,
        )

    def stat_start(i, carry):
        stat_copy(me, lax.rem(me + i, n_blk)).start()
        return carry

    def stat_wait(i, carry):
        peer = lax.rem(me + i, n_blk)
        stat_copy(peer, peer).wait_recv()
        return carry

    lax.fori_loop(1, n_blk, stat_start, 0)

    for k in range(2):

        def sent(origin, carry, k=k):
            @pl.when((origin <= place) & (place < length - 1))
            def _():
                line_copy(origin, k, gathered.at[origin, k], 1, right_send).wait_send()

            @pl.when((origin >= place) & (place > 0))
            def _():
                line_copy(origin, k, gathered.at[origin, k], -1, left_send).wait_send()

            return carry

        lax.fori_loop(0, length, sent, 0)

    def pool_sent(c, carry):
        cross_copy(c).wait_send()
        core_copy(my_row, c).wait_send()
        for peer in x_peers:
            x_copy(c, peer).wait_send()
            core_copy(peer, c).wait_send()
        return carry

    lax.fori_loop(0, CHUNKS, pool_sent, 0)
    for peer in row_peers:
        row_copy(my_row, peer).wait_send()
    for peer in row_peers + [my_row]:
        side_copy(my_row, peer).wait_send()

    lax.fori_loop(1, n_blk, stat_wait, 0)
    means = stats[:, 0, :]
    spreads = stats[:, 1, :]
    mean = jnp.sum(means, axis=0, keepdims=True) / n_blk
    spread = jnp.sum(spreads, axis=0, keepdims=True)
    spread = spread + rows * jnp.sum(jnp.square(means - mean), axis=0, keepdims=True)
    scale = jnp.sqrt(spread / (rows * n_blk) + 1e-05)
    mean_out[...] = jnp.broadcast_to(mean[:, 0:1], mean_out.shape)
    scale_out[...] = jnp.broadcast_to(scale[:, 0:1], scale_out.shape)

    def stat_sent(i, carry):
        stat_copy(me, lax.rem(me + i, n_blk)).wait_send()
        return carry

    lax.fori_loop(1, n_blk, stat_sent, 0)


def body(n_blk, n_row, pool_embeds, target_samples, reference_samples):
    rows, depth = pool_embeds.shape
    width = target_samples.shape[0]
    length = n_blk // 2
    dma = pltpu.SemaphoreType.DMA
    flops = 2 * rows * depth * 2 * width * n_blk
    log_target, log_ref, mean, scale = pl.pallas_call(
        functools.partial(density_kernel, n_blk, n_row),
        out_shape=[
            pltpu.VMEM((1, rows), jnp.float32),
            pltpu.VMEM((1, rows), jnp.float32),
            pltpu.VMEM((1, rows), jnp.float32),
            pltpu.VMEM((1, rows), jnp.float32),
        ],
        in_specs=[pl.BlockSpec(memory_space=pltpu.HBM)] * 3,
        out_specs=[pl.BlockSpec(memory_space=pltpu.VMEM)] * 4,
        scratch_shapes=[
            pltpu.VMEM((rows, depth), jnp.bfloat16),
            pltpu.VMEM((n_row, CHUNKS, rows // n_row // CHUNKS, depth), jnp.bfloat16),
            pltpu.VMEM((length, 2, width, depth), jnp.bfloat16),
            pltpu.VMEM((1, rows), jnp.float32),
            pltpu.VMEM((4, rows), jnp.float32),
            pltpu.VMEM((4, rows), jnp.float32),
            pltpu.VMEM((2 * n_row, 2, rows), jnp.float32),
            pltpu.VMEM((2, rows), jnp.float32),
            pltpu.VMEM((n_blk, 2, 128), jnp.float32),
            dma((3,)),
            dma((length, 2)),
            dma((length, 2)),
            dma((length, 2)),
            dma((CHUNKS,)),
            dma((n_row, CHUNKS)),
            dma((n_row, CHUNKS)),
            dma((n_row, CHUNKS)),
            dma((n_row,)),
            dma((n_row,)),
            dma((2 * n_row,)),
            dma((n_blk,)),
            dma((n_blk,)),
        ],
        compiler_params=pltpu.CompilerParams(
            collective_id=0, has_side_effects=True, vmem_limit_bytes=62 * 1024 * 1024
        ),
        cost_estimate=pl.CostEstimate(flops=flops, bytes_accessed=2 * rows * depth, transcendentals=0),
    )(pool_embeds, target_samples, reference_samples)
    ratio = log_target.reshape(rows) - log_ref.reshape(rows)
    return ratio, (ratio - mean.reshape(rows)) / scale.reshape(rows)


def solution(mesh):
    in_specs = (P("blk", None), P(("blk", "row"), None), P(("blk", "row"), None))
    out_specs = (P("blk"), P("blk"))
    part = functools.partial(body, mesh.shape["blk"], mesh.shape["row"])
    return jax.shard_map(part, mesh=mesh, in_specs=in_specs, out_specs=out_specs, check_vma=False)
```

```python
import functools
import math

import jax
import jax.numpy as jnp
from jax import lax
from jax.experimental import pallas as pl
from jax.experimental.pallas import tpu as pltpu
from jax.sharding import PartitionSpec as P

KERNEL_GAIN = 30.0
LOG2E = math.log2(math.e)
LN2 = math.log(2.0)
CHUNKS = 4
HALVES = 2
MESH = pl.DeviceIdType.MESH


def density_kernel(
    n_blk,
    n_row,
    pool_hbm,
    target_hbm,
    ref_hbm,
    target_out,
    ref_out,
    mean_out,
    scale_out,
    pools,
    gathered,
    pool_norms,
    high,
    total,
    partials,
    outgoing,
    stats,
    load_sem,
    right_send,
    left_send,
    line_recv,
    cross_send,
    x_send,
    core_send,
    pool_recv,
    row_send,
    side_send,
    part_recv,
    stat_send,
    stat_recv,
):
    me = lax.axis_index("blk")
    my_row = lax.axis_index("row")
    length = n_blk // 2
    place = me // 2
    other = me + 1 - 2 * lax.rem(me, 2)
    core = lax.rem(my_row, 2)
    core_peer = my_row + 1 - 2 * core
    x_peers = [lax.rem(my_row + 2 * j, n_row) for j in range(1, n_row // 2)]
    row_peers = [lax.rem(my_row + i, n_row) for i in range(1, n_row)]
    n_chunks = n_row * CHUNKS
    chunk, depth = pools.shape[2:]
    rows = n_chunks * chunk
    half = rows // HALVES
    per_half = n_chunks // HALVES
    width = target_hbm.shape[0]
    factor = KERNEL_GAIN / depth * LOG2E
    sources = (target_hbm, ref_hbm)
    nt = (((1,), (1,)), ((), ()))

    pool_load = pltpu.make_async_copy(pool_hbm, pools.at[0], load_sem.at[2])
    pool_load.start()
    own_loads = [
        pltpu.make_async_copy(sources[k], gathered.at[place, k], load_sem.at[k]) for k in range(2)
    ]
    for load in own_loads:
        load.start()

    barrier = pltpu.get_barrier_semaphore()

    near = pl.semaphore_signal

    @pl.when(place < length - 1)
    def _():
        near(barrier, inc=1, device_id={"blk": me + 2}, device_id_type=MESH)

    @pl.when(place > 0)
    def _():
        near(barrier, inc=1, device_id={"blk": me - 2}, device_id_type=MESH)

    near(barrier, inc=1, device_id={"blk": other}, device_id_type=MESH)
    for peer in x_peers + [core_peer]:
        near(barrier, inc=1, device_id={"row": peer}, device_id_type=MESH)
    ends = (place == 0).astype(jnp.int32) + (place == length - 1).astype(jnp.int32)
    pl.semaphore_wait(barrier, 4 + len(x_peers) - ends)

    def line_copy(origin, k, src, step, sems):
        return pltpu.make_async_remote_copy(
            src_ref=src,
            dst_ref=gathered.at[origin, k],
            send_sem=sems.at[origin, k],
            recv_sem=line_recv.at[origin, k],
            device_id={"blk": me + 2 * step},
            device_id_type=MESH,
        )

    def cross_copy(c):
        slot = c * n_row + my_row
        return pltpu.make_async_remote_copy(
            src_ref=pool_hbm.at[slot],
            dst_ref=pools.at[1, slot],
            send_sem=cross_send.at[c],
            recv_sem=pool_recv.at[my_row, c],
            device_id={"blk": other},
            device_id_type=MESH,
        )

    def row_relay(quarter, c, peer, send_sem):
        return pltpu.make_async_remote_copy(
            src_ref=pools.at[1, c * n_row + quarter],
            dst_ref=pools.at[1, c * n_row + quarter],
            send_sem=send_sem,
            recv_sem=pool_recv.at[quarter, c],
            device_id={"row": peer},
            device_id_type=MESH,
        )

    def core_copy(quarter, c):
        return row_relay(quarter, c, core_peer, core_send.at[quarter, c])

    def x_copy(c, peer):
        return row_relay(my_row, c, peer, x_send.at[peer, c])

    for k in range(2):

        @pl.when(place < length - 1)
        def _(k=k):
            line_copy(place, k, sources[k], 1, right_send).start()

        @pl.when(place > 0)
        def _(k=k):
            line_copy(place, k, sources[k], -1, left_send).start()

    for c in range(CHUNKS):
        cross_copy(c).start()

    high[...] = jnp.full_like(high, -1e30)
    total[...] = jnp.zeros_like(total)

    def fold(origin, which, part):
        block = gathered[origin].reshape(2 * width, depth)
        columns = pools[which, pl.ds(part * per_half, per_half)].reshape(half, depth)
        norms = jnp.sum(jnp.square(block.astype(jnp.float32)), axis=1, keepdims=True) * factor
        products = lax.dot_general(block, columns, nt, preferred_element_type=jnp.float32)
        scores_all = products * (2.0 * factor) - norms
        at = which * HALVES + part
        for k in range(2):
            scores = scores_all[width * k : width * (k + 1), :]
            old = high[at, k : k + 1, :]
            new = jnp.maximum(old, jnp.max(scores, axis=0, keepdims=True))
            summed = jnp.sum(jnp.exp2(scores - new), axis=0, keepdims=True)
            total[at, k : k + 1, :] = total[at, k : k + 1, :] * jnp.exp2(old - new) + summed
            high[at, k : k + 1, :] = new

    pool_load.wait()
    for load in own_loads:
        load.wait()

    ones = jnp.ones((8, depth), jnp.bfloat16)
    tile = n_row * chunk

    def norm_tile(i, carry):
        at = pl.multiple_of(i * tile, tile)
        block = pools[0, pl.ds(i * n_row, n_row)].reshape(tile, depth)
        squares = jnp.square(block.astype(jnp.float32))
        coarse = squares.astype(jnp.bfloat16)
        fine = (squares - coarse.astype(jnp.float32)).astype(jnp.bfloat16)
        sums = lax.dot_general(ones, coarse, nt, preferred_element_type=jnp.float32)
        sums = sums + lax.dot_general(ones, fine, nt, preferred_element_type=jnp.float32)
        pool_norms[:, pl.ds(at, tile)] = sums[0:1, :] * factor
        return carry

    line_ticks = 2 * (length - 1)
    ticks = max(line_ticks, CHUNKS + 2)

    def tick(i, carry):
        step = i // 2 + 1
        k = lax.rem(i, 2)

        @pl.when((i < line_ticks) & (place >= step))
        def _():
            origin = place - step
            block = gathered.at[origin, k]
            line_copy(origin, k, block, 1, right_send).wait_recv()

            @pl.when(place < length - 1)
            def _():
                line_copy(origin, k, block, 1, right_send).start()

        @pl.when((i < line_ticks) & (place + step < length))
        def _():
            origin = place + step
            block = gathered.at[origin, k]
            line_copy(origin, k, block, -1, left_send).wait_recv()

            @pl.when(place > 0)
            def _():
                line_copy(origin, k, block, -1, left_send).start()

        @pl.when(i < CHUNKS)
        def _():
            cross_copy(i).wait_recv()
            for peer in x_peers:
                x_copy(i, peer).start()
            core_copy(my_row, i).start()

        @pl.when((i >= 1) & (i <= CHUNKS))
        def _():
            for peer in x_peers:
                row_relay(peer, i - 1, peer, x_send.at[peer, i - 1]).wait_recv()
                core_copy(peer, i - 1).start()

        @pl.when(i < rows // tile)
        def _():
            norm_tile(i, 0)

        for part in range(HALVES):

            @pl.when(i == ticks - 1 - HALVES + part)
            def _(part=part):
                def arrived(c, carry):
                    for j in range(n_row // 2):
                        core_copy(lax.rem(core_peer + 2 * j, n_row), c).wait_recv()
                    return carry

                each = CHUNKS // HALVES
                lax.fori_loop(part * each, (part + 1) * each, arrived, 0)

        def job(j, carry):
            origin = lax.rem(j // HALVES, length)
            part = lax.rem(j, HALVES)
            which = j // (HALVES * length)
            apart = jnp.maximum(origin - place, place - origin)
            own_turn = jnp.maximum(2 * apart - 1, 0)
            other_turn = jnp.where(apart < length - 1, ticks - 1 - HALVES + part, ticks - 1)
            turn = jnp.where(which == 0, own_turn, other_turn)

            @pl.when(turn == i)
            def _():
                fold(origin, which, part)

            return carry

        lax.fori_loop(0, 2 * length * HALVES, job, 0)
        return carry

    lax.fori_loop(0, ticks, tick, 0)
    lax.fori_loop(ticks, max(ticks, rows // tile), norm_tile, 0)

    logs = (high[...] + jnp.log2(total[...])) * LN2
    partials[my_row] = jnp.concatenate([logs[i] for i in range(HALVES)], axis=1)
    outgoing[...] = jnp.concatenate([logs[HALVES + i] for i in range(HALVES)], axis=1)

    def row_copy(slot, peer):
        return pltpu.make_async_remote_copy(
            src_ref=partials.at[slot],
            dst_ref=partials.at[slot],
            send_sem=row_send.at[peer],
            recv_sem=part_recv.at[slot],
            device_id={"row": peer},
            device_id_type=MESH,
        )

    def side_copy(row, peer):
        return pltpu.make_async_remote_copy(
            src_ref=outgoing,
            dst_ref=partials.at[n_row + row],
            send_sem=side_send.at[peer],
            recv_sem=part_recv.at[n_row + row],
            device_id={"blk": other, "row": peer},
            device_id_type=MESH,
        )

    for peer in row_peers + [my_row]:
        side_copy(my_row, peer).start()
    for peer in row_peers:
        row_copy(my_row, peer).start()
    for peer in row_peers:
        row_copy(peer, peer).wait_recv()
    for peer in row_peers + [my_row]:
        side_copy(peer, peer).wait_recv()
    parts = [partials[i] for i in range(2 * n_row)]
    top = functools.reduce(jnp.maximum, parts)
    mass = functools.reduce(jnp.add, [jnp.exp(part - top) for part in parts])
    logs = top + jnp.log(mass) - pool_norms[...] * LN2
    ratio = logs[0:1, :] - logs[1:2, :]
    target_out[...] = logs[0:1, :]
    ref_out[...] = logs[1:2, :]

    local_mean = jnp.sum(ratio, axis=1, keepdims=True) / rows
    local_spread = jnp.sum(jnp.square(ratio - local_mean), axis=1, keepdims=True)
    lanes = stats.shape[2]
    stats[me, 0:1, :] = jnp.broadcast_to(local_mean, (1, lanes))
    stats[me, 1:2, :] = jnp.broadcast_to(local_spread, (1, lanes))

    def stat_copy(slot, peer):
        return pltpu.make_async_remote_copy(
            src_ref=stats.at[slot],
            dst_ref=stats.at[slot],
            send_sem=stat_send.at[peer],
            recv_sem=stat_recv.at[slot],
            device_id={"blk": peer},
            device_id_type=MESH,
        )

    def stat_start(i, carry):
        stat_copy(me, lax.rem(me + i, n_blk)).start()
        return carry

    def stat_wait(i, carry):
        peer = lax.rem(me + i, n_blk)
        stat_copy(peer, peer).wait_recv()
        return carry

    lax.fori_loop(1, n_blk, stat_start, 0)

    for k in range(2):

        def sent(origin, carry, k=k):
            @pl.when((origin <= place) & (place < length - 1))
            def _():
                line_copy(origin, k, gathered.at[origin, k], 1, right_send).wait_send()

            @pl.when((origin >= place) & (place > 0))
            def _():
                line_copy(origin, k, gathered.at[origin, k], -1, left_send).wait_send()

            return carry

        lax.fori_loop(0, length, sent, 0)

    def pool_sent(c, carry):
        cross_copy(c).wait_send()
        core_copy(my_row, c).wait_send()
        for peer in x_peers:
            x_copy(c, peer).wait_send()
            core_copy(peer, c).wait_send()
        return carry

    lax.fori_loop(0, CHUNKS, pool_sent, 0)
    for peer in row_peers:
        row_copy(my_row, peer).wait_send()
    for peer in row_peers + [my_row]:
        side_copy(my_row, peer).wait_send()

    lax.fori_loop(1, n_blk, stat_wait, 0)
    means = stats[:, 0, :]
    spreads = stats[:, 1, :]
    mean = jnp.sum(means, axis=0, keepdims=True) / n_blk
    spread = jnp.sum(spreads, axis=0, keepdims=True)
    spread = spread + rows * jnp.sum(jnp.square(means - mean), axis=0, keepdims=True)
    scale = jnp.sqrt(spread / (rows * n_blk) + 1e-05)
    mean_out[...] = jnp.broadcast_to(mean[:, 0:1], mean_out.shape)
    scale_out[...] = jnp.broadcast_to(scale[:, 0:1], scale_out.shape)

    def stat_sent(i, carry):
        stat_copy(me, lax.rem(me + i, n_blk)).wait_send()
        return carry

    lax.fori_loop(1, n_blk, stat_sent, 0)


def body(n_blk, n_row, pool_embeds, target_samples, reference_samples):
    rows, depth = pool_embeds.shape
    width = target_samples.shape[0]
    length = n_blk // 2
    chunk = rows // (n_row * CHUNKS)
    dma = pltpu.SemaphoreType.DMA
    flops = 2 * rows * depth * 2 * width * n_blk
    log_target, log_ref, mean, scale = pl.pallas_call(
        functools.partial(density_kernel, n_blk, n_row),
        out_shape=[
            pltpu.VMEM((1, rows), jnp.float32),
            pltpu.VMEM((1, rows), jnp.float32),
            pltpu.VMEM((1, rows), jnp.float32),
            pltpu.VMEM((1, rows), jnp.float32),
        ],
        in_specs=[pl.BlockSpec(memory_space=pltpu.HBM)] * 3,
        out_specs=[pl.BlockSpec(memory_space=pltpu.VMEM)] * 4,
        scratch_shapes=[
            pltpu.VMEM((2, n_row * CHUNKS, chunk, depth), jnp.bfloat16),
            pltpu.VMEM((length, 2, width, depth), jnp.bfloat16),
            pltpu.VMEM((1, rows), jnp.float32),
            pltpu.VMEM((2 * HALVES, 2, rows // HALVES), jnp.float32),
            pltpu.VMEM((2 * HALVES, 2, rows // HALVES), jnp.float32),
            pltpu.VMEM((2 * n_row, 2, rows), jnp.float32),
            pltpu.VMEM((2, rows), jnp.float32),
            pltpu.VMEM((n_blk, 2, 128), jnp.float32),
            dma((3,)),
            dma((length, 2)),
            dma((length, 2)),
            dma((length, 2)),
            dma((CHUNKS,)),
            dma((n_row, CHUNKS)),
            dma((n_row, CHUNKS)),
            dma((n_row, CHUNKS)),
            dma((n_row,)),
            dma((n_row,)),
            dma((2 * n_row,)),
            dma((n_blk,)),
            dma((n_blk,)),
        ],
        compiler_params=pltpu.CompilerParams(
            collective_id=0, has_side_effects=True, vmem_limit_bytes=62 * 1024 * 1024
        ),
        cost_estimate=pl.CostEstimate(flops=flops, bytes_accessed=2 * rows * depth, transcendentals=0),
    )(pool_embeds.reshape(n_row * CHUNKS, chunk, depth), target_samples, reference_samples)
    ratio = log_target.reshape(rows) - log_ref.reshape(rows)
    return ratio, (ratio - mean.reshape(rows)) / scale.reshape(rows)


def solution(mesh):
    in_specs = (P("blk", None), P(("blk", "row"), None), P(("blk", "row"), None))
    out_specs = (P("blk"), P("blk"))
    part = functools.partial(body, mesh.shape["blk"], mesh.shape["row"])
    return jax.shard_map(part, mesh=mesh, in_specs=in_specs, out_specs=out_specs, check_vma=False)
```

```python
import functools
import math

import jax
import jax.numpy as jnp
from jax import lax
from jax.experimental import pallas as pl
from jax.experimental.pallas import tpu as pltpu
from jax.sharding import PartitionSpec as P

KERNEL_GAIN = 30.0
LOG2E = math.log2(math.e)
LN2 = math.log(2.0)
CHUNKS = 4
MESH = pl.DeviceIdType.MESH


def density_kernel(
    n_blk,
    n_row,
    pool_hbm,
    target_hbm,
    ref_hbm,
    target_out,
    ref_out,
    mean_out,
    scale_out,
    pool,
    other_pool,
    gathered,
    pool_norms,
    sample_norms,
    high,
    total,
    partials,
    outgoing,
    stats,
    load_sem,
    right_send,
    left_send,
    line_recv,
    cross_send,
    x_send,
    core_send,
    pool_recv,
    row_send,
    side_send,
    part_recv,
    stat_send,
    stat_recv,
):
    me = lax.axis_index("blk")
    my_row = lax.axis_index("row")
    length = n_blk // 2
    place = me // 2
    other = me + 1 - 2 * lax.rem(me, 2)
    core = lax.rem(my_row, 2)
    core_peer = my_row + 1 - 2 * core
    x_peers = [lax.rem(my_row + 2 * j, n_row) for j in range(1, n_row // 2)]
    row_peers = [lax.rem(my_row + i, n_row) for i in range(1, n_row)]
    rows, depth = pool.shape
    lanes = stats.shape[2]
    width = target_hbm.shape[0]
    chunk = other_pool.shape[2]
    factor = KERNEL_GAIN / depth * LOG2E
    sources = (target_hbm, ref_hbm)
    nt = (((1,), (1,)), ((), ()))

    pool_load = pltpu.make_async_copy(pool_hbm, pool, load_sem.at[2])
    pool_load.start()
    own_loads = [
        pltpu.make_async_copy(sources[k], gathered.at[place, k], load_sem.at[k]) for k in range(2)
    ]
    for load in own_loads:
        load.start()

    barrier = pltpu.get_barrier_semaphore()

    near = pl.semaphore_signal

    @pl.when(place < length - 1)
    def _():
        near(barrier, inc=1, device_id={"blk": me + 2}, device_id_type=MESH)

    @pl.when(place > 0)
    def _():
        near(barrier, inc=1, device_id={"blk": me - 2}, device_id_type=MESH)

    near(barrier, inc=1, device_id={"blk": other}, device_id_type=MESH)
    for peer in x_peers + [core_peer]:
        near(barrier, inc=1, device_id={"row": peer}, device_id_type=MESH)
    ends = (place == 0).astype(jnp.int32) + (place == length - 1).astype(jnp.int32)
    pl.semaphore_wait(barrier, 4 + len(x_peers) - ends)

    def line_copy(origin, k, src, step, sems):
        return pltpu.make_async_remote_copy(
            src_ref=src,
            dst_ref=gathered.at[origin, k],
            send_sem=sems.at[origin, k],
            recv_sem=line_recv.at[origin, k],
            device_id={"blk": me + 2 * step},
            device_id_type=MESH,
        )

    def cross_copy(c):
        at = pl.multiple_of((my_row * CHUNKS + c) * chunk, chunk)
        return pltpu.make_async_remote_copy(
            src_ref=pool_hbm.at[pl.ds(at, chunk)],
            dst_ref=other_pool.at[my_row, c],
            send_sem=cross_send.at[c],
            recv_sem=pool_recv.at[my_row, c],
            device_id={"blk": other},
            device_id_type=MESH,
        )

    def row_relay(quarter, c, peer, send_sem):
        return pltpu.make_async_remote_copy(
            src_ref=other_pool.at[quarter, c],
            dst_ref=other_pool.at[quarter, c],
            send_sem=send_sem,
            recv_sem=pool_recv.at[quarter, c],
            device_id={"row": peer},
            device_id_type=MESH,
        )

    def core_copy(quarter, c):
        return row_relay(quarter, c, core_peer, core_send.at[quarter, c])

    def x_copy(c, peer):
        return row_relay(my_row, c, peer, x_send.at[peer, c])

    for k in range(2):

        @pl.when(place < length - 1)
        def _(k=k):
            line_copy(place, k, sources[k], 1, right_send).start()

        @pl.when(place > 0)
        def _(k=k):
            line_copy(place, k, sources[k], -1, left_send).start()

    for c in range(CHUNKS):
        cross_copy(c).start()

    high[...] = jnp.full_like(high, -1e30)
    total[...] = jnp.zeros_like(total)

    def set_norms(origin, k):
        block = gathered[origin, k].astype(jnp.float32)
        norms = jnp.sum(jnp.square(block), axis=1, keepdims=True) * factor
        sample_norms[origin, k] = jnp.broadcast_to(norms, (width, lanes))

    def fold(origin, which, count=1):
        block = gathered[pl.ds(origin, count)].reshape(count * 2 * width, depth)
        columns = pool[...] if which == 0 else other_pool[...].reshape(rows, depth)
        norms = sample_norms[pl.ds(origin, count)].reshape(count * 2 * width, lanes)
        norms = jnp.concatenate([norms] * (rows // lanes), axis=1)
        products = lax.dot_general(block, columns, nt, preferred_element_type=jnp.float32)
        scores_all = products * (2.0 * factor) - norms
        for k in range(2):
            pieces = [scores_all[(2 * j + k) * width : (2 * j + k + 1) * width, :] for j in range(count)]
            at = 2 * which + k
            old = high[at : at + 1, :]
            best = [jnp.max(piece, axis=0, keepdims=True) for piece in pieces]
            new = functools.reduce(jnp.maximum, best, old)
            sums = [jnp.sum(jnp.exp2(piece - new), axis=0, keepdims=True) for piece in pieces]
            total[at : at + 1, :] = total[at : at + 1, :] * jnp.exp2(old - new) + sum(sums)
            high[at : at + 1, :] = new

    pool_load.wait()
    for load in own_loads:
        load.wait()
    for k in range(2):
        set_norms(place, k)
    fold(place, 0)

    ones = jnp.ones((8, depth), jnp.bfloat16)
    tile = 256 if rows % 256 == 0 else rows

    def norm_tile(i, carry):
        at = pl.multiple_of(i * tile, tile)
        squares = jnp.square(pool[pl.ds(at, tile), :].astype(jnp.float32))
        coarse = squares.astype(jnp.bfloat16)
        fine = (squares - coarse.astype(jnp.float32)).astype(jnp.bfloat16)
        sums = lax.dot_general(ones, coarse, nt, preferred_element_type=jnp.float32)
        sums = sums + lax.dot_general(ones, fine, nt, preferred_element_type=jnp.float32)
        pool_norms[:, pl.ds(at, tile)] = sums[0:1, :] * factor
        return carry

    line_ticks = 2 * (length - 1)
    ticks = max(line_ticks, CHUNKS + 2)

    def tick(i, carry):
        step = i // 2 + 1
        k = lax.rem(i, 2)

        @pl.when((i < line_ticks) & (place >= step))
        def _():
            origin = place - step
            block = gathered.at[origin, k]
            line_copy(origin, k, block, 1, right_send).wait_recv()

            @pl.when(place < length - 1)
            def _():
                line_copy(origin, k, block, 1, right_send).start()

        @pl.when((i < line_ticks) & (place + step < length))
        def _():
            origin = place + step
            block = gathered.at[origin, k]
            line_copy(origin, k, block, -1, left_send).wait_recv()

            @pl.when(place > 0)
            def _():
                line_copy(origin, k, block, -1, left_send).start()

        @pl.when(i < CHUNKS)
        def _():
            cross_copy(i).wait_recv()
            for peer in x_peers:
                x_copy(i, peer).start()
            core_copy(my_row, i).start()

        @pl.when((i >= 1) & (i <= CHUNKS))
        def _():
            for peer in x_peers:
                row_relay(peer, i - 1, peer, x_send.at[peer, i - 1]).wait_recv()
                core_copy(peer, i - 1).start()

        @pl.when(i < rows // tile)
        def _():
            norm_tile(i, 0)

        def norms_of(j, carry):
            origin = place + (2 * j - 1) * step

            @pl.when((i < line_ticks) & (origin >= 0) & (origin < length))
            def _():
                set_norms(origin, k)

            return carry

        lax.fori_loop(0, 2, norms_of, 0)

        @pl.when((k == 1) & (place >= step) & (i < line_ticks - 1))
        def _():
            fold(place - step, 0)

        @pl.when((k == 1) & (place + step < length) & (i < line_ticks - 1))
        def _():
            fold(place + step, 0)

        @pl.when(i == ticks - 2)
        def _():
            for j in range(n_row // 2):
                quarter = lax.rem(core_peer + 2 * j, n_row)

                def arrived(c, carry, quarter=quarter):
                    core_copy(quarter, c).wait_recv()
                    return carry

                lax.fori_loop(0, CHUNKS, arrived, 0)

            first = jnp.minimum(place, 1)
            if length <= 4:
                fold(first, 1, length - 1)
            else:

                def early(origin, carry):
                    fold(origin, 1)
                    return carry

                lax.fori_loop(first, first + length - 1, early, 0)

            @pl.when((place > 0) & (place < length - 1))
            def _():
                fold(0, 1)

        return carry

    lax.fori_loop(0, ticks, tick, 0)
    lax.fori_loop(ticks, max(ticks, rows // tile), norm_tile, 0)

    @pl.when((place == 0) | (place == length - 1))
    def _():
        last = length - 1 - place
        fold(last, 0)
        fold(last, 1)

    logs = (high[...] + jnp.log2(total[...])) * LN2
    partials[my_row] = logs[0:2, :]
    outgoing[...] = logs[2:4, :]

    def row_copy(slot, peer):
        return pltpu.make_async_remote_copy(
            src_ref=partials.at[slot],
            dst_ref=partials.at[slot],
            send_sem=row_send.at[peer],
            recv_sem=part_recv.at[slot],
            device_id={"row": peer},
            device_id_type=MESH,
        )

    def side_copy(row, peer):
        return pltpu.make_async_remote_copy(
            src_ref=outgoing,
            dst_ref=partials.at[n_row + row],
            send_sem=side_send.at[peer],
            recv_sem=part_recv.at[n_row + row],
            device_id={"blk": other, "row": peer},
            device_id_type=MESH,
        )

    for peer in row_peers + [my_row]:
        side_copy(my_row, peer).start()
    for peer in row_peers:
        row_copy(my_row, peer).start()
    for peer in row_peers:
        row_copy(peer, peer).wait_recv()
    for peer in row_peers + [my_row]:
        side_copy(peer, peer).wait_recv()
    parts = [partials[i] for i in range(2 * n_row)]
    top = functools.reduce(jnp.maximum, parts)
    mass = functools.reduce(jnp.add, [jnp.exp(part - top) for part in parts])
    logs = top + jnp.log(mass) - pool_norms[...] * LN2
    ratio = logs[0:1, :] - logs[1:2, :]
    target_out[...] = logs[0:1, :]
    ref_out[...] = logs[1:2, :]

    local_mean = jnp.sum(ratio, axis=1, keepdims=True) / rows
    local_spread = jnp.sum(jnp.square(ratio - local_mean), axis=1, keepdims=True)
    stats[me, 0:1, :] = jnp.broadcast_to(local_mean, (1, lanes))
    stats[me, 1:2, :] = jnp.broadcast_to(local_spread, (1, lanes))

    def stat_copy(slot, peer):
        return pltpu.make_async_remote_copy(
            src_ref=stats.at[slot],
            dst_ref=stats.at[slot],
            send_sem=stat_send.at[peer],
            recv_sem=stat_recv.at[slot],
            device_id={"blk": peer},
            device_id_type=MESH,
        )

    def stat_start(i, carry):
        stat_copy(me, lax.rem(me + i, n_blk)).start()
        return carry

    def stat_wait(i, carry):
        peer = lax.rem(me + i, n_blk)
        stat_copy(peer, peer).wait_recv()
        return carry

    lax.fori_loop(1, n_blk, stat_start, 0)

    for k in range(2):

        def sent(origin, carry, k=k):
            @pl.when((origin <= place) & (place < length - 1))
            def _():
                line_copy(origin, k, gathered.at[origin, k], 1, right_send).wait_send()

            @pl.when((origin >= place) & (place > 0))
            def _():
                line_copy(origin, k, gathered.at[origin, k], -1, left_send).wait_send()

            return carry

        lax.fori_loop(0, length, sent, 0)

    def pool_sent(c, carry):
        cross_copy(c).wait_send()
        core_copy(my_row, c).wait_send()
        for peer in x_peers:
            x_copy(c, peer).wait_send()
            core_copy(peer, c).wait_send()
        return carry

    lax.fori_loop(0, CHUNKS, pool_sent, 0)
    for peer in row_peers:
        row_copy(my_row, peer).wait_send()
    for peer in row_peers + [my_row]:
        side_copy(my_row, peer).wait_send()

    lax.fori_loop(1, n_blk, stat_wait, 0)
    means = stats[:, 0, :]
    spreads = stats[:, 1, :]
    mean = jnp.sum(means, axis=0, keepdims=True) / n_blk
    spread = jnp.sum(spreads, axis=0, keepdims=True)
    spread = spread + rows * jnp.sum(jnp.square(means - mean), axis=0, keepdims=True)
    scale = jnp.sqrt(spread / (rows * n_blk) + 1e-05)
    mean_out[...] = jnp.broadcast_to(mean[:, 0:1], mean_out.shape)
    scale_out[...] = jnp.broadcast_to(scale[:, 0:1], scale_out.shape)

    def stat_sent(i, carry):
        stat_copy(me, lax.rem(me + i, n_blk)).wait_send()
        return carry

    lax.fori_loop(1, n_blk, stat_sent, 0)


def body(n_blk, n_row, pool_embeds, target_samples, reference_samples):
    rows, depth = pool_embeds.shape
    width = target_samples.shape[0]
    length = n_blk // 2
    dma = pltpu.SemaphoreType.DMA
    flops = 2 * rows * depth * 2 * width * n_blk
    log_target, log_ref, mean, scale = pl.pallas_call(
        functools.partial(density_kernel, n_blk, n_row),
        out_shape=[
            pltpu.VMEM((1, rows), jnp.float32),
            pltpu.VMEM((1, rows), jnp.float32),
            pltpu.VMEM((1, rows), jnp.float32),
            pltpu.VMEM((1, rows), jnp.float32),
        ],
        in_specs=[pl.BlockSpec(memory_space=pltpu.HBM)] * 3,
        out_specs=[pl.BlockSpec(memory_space=pltpu.VMEM)] * 4,
        scratch_shapes=[
            pltpu.VMEM((rows, depth), jnp.bfloat16),
            pltpu.VMEM((n_row, CHUNKS, rows // n_row // CHUNKS, depth), jnp.bfloat16),
            pltpu.VMEM((length, 2, width, depth), jnp.bfloat16),
            pltpu.VMEM((1, rows), jnp.float32),
            pltpu.VMEM((length, 2, width, 128), jnp.float32),
            pltpu.VMEM((4, rows), jnp.float32),
            pltpu.VMEM((4, rows), jnp.float32),
            pltpu.VMEM((2 * n_row, 2, rows), jnp.float32),
            pltpu.VMEM((2, rows), jnp.float32),
            pltpu.VMEM((n_blk, 2, 128), jnp.float32),
            dma((3,)),
            dma((length, 2)),
            dma((length, 2)),
            dma((length, 2)),
            dma((CHUNKS,)),
            dma((n_row, CHUNKS)),
            dma((n_row, CHUNKS)),
            dma((n_row, CHUNKS)),
            dma((n_row,)),
            dma((n_row,)),
            dma((2 * n_row,)),
            dma((n_blk,)),
            dma((n_blk,)),
        ],
        compiler_params=pltpu.CompilerParams(
            collective_id=0, has_side_effects=True, vmem_limit_bytes=62 * 1024 * 1024
        ),
        cost_estimate=pl.CostEstimate(flops=flops, bytes_accessed=2 * rows * depth, transcendentals=0),
    )(pool_embeds, target_samples, reference_samples)
    ratio = log_target.reshape(rows) - log_ref.reshape(rows)
    return ratio, (ratio - mean.reshape(rows)) / scale.reshape(rows)


def solution(mesh):
    in_specs = (P("blk", None), P(("blk", "row"), None), P(("blk", "row"), None))
    out_specs = (P("blk"), P("blk"))
    part = functools.partial(body, mesh.shape["blk"], mesh.shape["row"])
    return jax.shard_map(part, mesh=mesh, in_specs=in_specs, out_specs=out_specs, check_vma=False)
```

```python
import functools
import math

import jax
import jax.numpy as jnp
from jax import lax
from jax.experimental import pallas as pl
from jax.experimental.pallas import tpu as pltpu
from jax.sharding import PartitionSpec as P

KERNEL_GAIN = 30.0
LOG2E = math.log2(math.e)
LN2 = math.log(2.0)
CHUNKS = 4
MESH = pl.DeviceIdType.MESH


def density_kernel(
    n_blk,
    n_row,
    pool_hbm,
    target_hbm,
    ref_hbm,
    target_out,
    ref_out,
    mean_out,
    scale_out,
    pool,
    other_pool,
    gathered,
    pool_norms,
    sample_norms,
    high,
    total,
    partials,
    outgoing,
    stats,
    load_sem,
    right_send,
    left_send,
    line_recv,
    cross_send,
    x_send,
    core_send,
    pool_recv,
    row_send,
    side_send,
    part_recv,
    stat_send,
    stat_recv,
):
    me = lax.axis_index("blk")
    my_row = lax.axis_index("row")
    length = n_blk // 2
    place = me // 2
    other = me + 1 - 2 * lax.rem(me, 2)
    core = lax.rem(my_row, 2)
    core_peer = my_row + 1 - 2 * core
    x_peers = [lax.rem(my_row + 2 * j, n_row) for j in range(1, n_row // 2)]
    row_peers = [lax.rem(my_row + i, n_row) for i in range(1, n_row)]
    rows, depth = pool.shape
    lanes = stats.shape[2]
    width = target_hbm.shape[0]
    chunk = other_pool.shape[2]
    factor = KERNEL_GAIN / depth * LOG2E
    sources = (target_hbm, ref_hbm)
    nt = (((1,), (1,)), ((), ()))

    pool_load = pltpu.make_async_copy(pool_hbm, pool, load_sem.at[2])
    pool_load.start()
    own_loads = [
        pltpu.make_async_copy(sources[k], gathered.at[place, k], load_sem.at[k]) for k in range(2)
    ]
    for load in own_loads:
        load.start()

    barrier = pltpu.get_barrier_semaphore()

    near = pl.semaphore_signal

    @pl.when(place < length - 1)
    def _():
        near(barrier, inc=1, device_id={"blk": me + 2}, device_id_type=MESH)

    @pl.when(place > 0)
    def _():
        near(barrier, inc=1, device_id={"blk": me - 2}, device_id_type=MESH)

    near(barrier, inc=1, device_id={"blk": other}, device_id_type=MESH)
    for peer in x_peers + [core_peer]:
        near(barrier, inc=1, device_id={"row": peer}, device_id_type=MESH)
    ends = (place == 0).astype(jnp.int32) + (place == length - 1).astype(jnp.int32)
    pl.semaphore_wait(barrier, 4 + len(x_peers) - ends)

    def line_copy(origin, k, src, step, sems):
        return pltpu.make_async_remote_copy(
            src_ref=src,
            dst_ref=gathered.at[origin, k],
            send_sem=sems.at[origin, k],
            recv_sem=line_recv.at[origin, k],
            device_id={"blk": me + 2 * step},
            device_id_type=MESH,
        )

    def cross_copy(c):
        at = pl.multiple_of((my_row * CHUNKS + c) * chunk, chunk)
        return pltpu.make_async_remote_copy(
            src_ref=pool_hbm.at[pl.ds(at, chunk)],
            dst_ref=other_pool.at[my_row, c],
            send_sem=cross_send.at[c],
            recv_sem=pool_recv.at[my_row, c],
            device_id={"blk": other},
            device_id_type=MESH,
        )

    def row_relay(quarter, c, peer, send_sem):
        return pltpu.make_async_remote_copy(
            src_ref=other_pool.at[quarter, c],
            dst_ref=other_pool.at[quarter, c],
            send_sem=send_sem,
            recv_sem=pool_recv.at[quarter, c],
            device_id={"row": peer},
            device_id_type=MESH,
        )

    def core_copy(quarter, c):
        return row_relay(quarter, c, core_peer, core_send.at[quarter, c])

    def x_copy(c, peer):
        return row_relay(my_row, c, peer, x_send.at[peer, c])

    for k in range(2):

        @pl.when(place < length - 1)
        def _(k=k):
            line_copy(place, k, sources[k], 1, right_send).start()

        @pl.when(place > 0)
        def _(k=k):
            line_copy(place, k, sources[k], -1, left_send).start()

    for c in range(CHUNKS):
        cross_copy(c).start()

    high[...] = jnp.full_like(high, -1e30)
    total[...] = jnp.zeros_like(total)

    def set_norms(origin, k):
        block = gathered[origin, k].astype(jnp.float32)
        norms = jnp.sum(jnp.square(block), axis=1, keepdims=True) * factor
        sample_norms[origin, k] = jnp.broadcast_to(norms, (width, lanes))

    def fold(origin, which, count=1):
        block = gathered[pl.ds(origin, count)].reshape(count * 2 * width, depth)
        columns = pool[...] if which == 0 else other_pool[...].reshape(rows, depth)
        norms = sample_norms[pl.ds(origin, count)].reshape(count * 2 * width, lanes)
        norms = jnp.concatenate([norms] * (rows // lanes), axis=1)
        products = lax.dot_general(block, columns, nt, preferred_element_type=jnp.float32)
        scores_all = products * (2.0 * factor) - norms
        for k in range(2):
            pieces = [scores_all[(2 * j + k) * width : (2 * j + k + 1) * width, :] for j in range(count)]
            at = 2 * which + k
            old = high[at : at + 1, :]
            best = [jnp.max(piece, axis=0, keepdims=True) for piece in pieces]
            new = functools.reduce(jnp.maximum, best, old)
            sums = [jnp.sum(jnp.exp2(piece - new), axis=0, keepdims=True) for piece in pieces]
            total[at : at + 1, :] = total[at : at + 1, :] * jnp.exp2(old - new) + sum(sums)
            high[at : at + 1, :] = new

    pool_load.wait()
    for load in own_loads:
        load.wait()
    def fold_early(which):
        middle = (place > 0) & (place < length - 1)
        first = jnp.minimum(place, 1)
        if length <= 4:

            @pl.when(middle)
            def _():
                fold(0, which, length)

            @pl.when(jnp.logical_not(middle))
            def _():
                fold(first, which, length - 1)

        else:

            def early(origin, carry):
                fold(origin, which)
                return carry

            stop = first + length - 1
            lax.fori_loop(jnp.where(middle, 0, first), stop, early, 0)

    ones = jnp.ones((8, depth), jnp.bfloat16)
    tile = 256 if rows % 256 == 0 else rows

    def norm_tile(i, carry):
        at = pl.multiple_of(i * tile, tile)
        squares = jnp.square(pool[pl.ds(at, tile), :].astype(jnp.float32))
        coarse = squares.astype(jnp.bfloat16)
        fine = (squares - coarse.astype(jnp.float32)).astype(jnp.bfloat16)
        sums = lax.dot_general(ones, coarse, nt, preferred_element_type=jnp.float32)
        sums = sums + lax.dot_general(ones, fine, nt, preferred_element_type=jnp.float32)
        pool_norms[:, pl.ds(at, tile)] = sums[0:1, :] * factor
        return carry

    lax.fori_loop(0, rows // tile, norm_tile, 0)
    line_ticks = 2 * (length - 1)
    ticks = max(line_ticks, CHUNKS + 2)

    def tick(i, carry):
        step = i // 2 + 1
        k = lax.rem(i, 2)

        @pl.when((i < line_ticks) & (place >= step))
        def _():
            origin = place - step
            block = gathered.at[origin, k]
            line_copy(origin, k, block, 1, right_send).wait_recv()

            @pl.when(place < length - 1)
            def _():
                line_copy(origin, k, block, 1, right_send).start()

        @pl.when((i < line_ticks) & (place + step < length))
        def _():
            origin = place + step
            block = gathered.at[origin, k]
            line_copy(origin, k, block, -1, left_send).wait_recv()

            @pl.when(place > 0)
            def _():
                line_copy(origin, k, block, -1, left_send).start()

        @pl.when(i < CHUNKS)
        def _():
            cross_copy(i).wait_recv()
            for peer in x_peers:
                x_copy(i, peer).start()
            core_copy(my_row, i).start()

        @pl.when((i >= 1) & (i <= CHUNKS))
        def _():
            for peer in x_peers:
                row_relay(peer, i - 1, peer, x_send.at[peer, i - 1]).wait_recv()
                core_copy(peer, i - 1).start()

        @pl.when(i == ticks - 3)
        def _():
            def all_norms(j, carry):
                origin = j // 2

                @pl.when((origin - place < length - 1) & (place - origin < length - 1))
                def _():
                    set_norms(origin, lax.rem(j, 2))

                return carry

            lax.fori_loop(0, 2 * length, all_norms, 0)
            fold_early(0)

        @pl.when(i == ticks - 2)
        def _():
            for j in range(n_row // 2):
                quarter = lax.rem(core_peer + 2 * j, n_row)

                def arrived(c, carry, quarter=quarter):
                    core_copy(quarter, c).wait_recv()
                    return carry

                lax.fori_loop(0, CHUNKS, arrived, 0)

            fold_early(1)

        @pl.when((i >= line_ticks - 2) & (i < line_ticks) & ((place == 0) | (place == length - 1)))
        def _():
            set_norms(length - 1 - place, k)

        return carry

    lax.fori_loop(0, ticks, tick, 0)

    @pl.when((place == 0) | (place == length - 1))
    def _():
        last = length - 1 - place
        fold(last, 0)
        fold(last, 1)

    logs = (high[...] + jnp.log2(total[...])) * LN2
    partials[my_row] = logs[0:2, :]
    outgoing[...] = logs[2:4, :]

    def row_copy(slot, peer):
        return pltpu.make_async_remote_copy(
            src_ref=partials.at[slot],
            dst_ref=partials.at[slot],
            send_sem=row_send.at[peer],
            recv_sem=part_recv.at[slot],
            device_id={"row": peer},
            device_id_type=MESH,
        )

    def side_copy(row, peer):
        return pltpu.make_async_remote_copy(
            src_ref=outgoing,
            dst_ref=partials.at[n_row + row],
            send_sem=side_send.at[peer],
            recv_sem=part_recv.at[n_row + row],
            device_id={"blk": other, "row": peer},
            device_id_type=MESH,
        )

    for peer in row_peers + [my_row]:
        side_copy(my_row, peer).start()
    for peer in row_peers:
        row_copy(my_row, peer).start()
    for peer in row_peers:
        row_copy(peer, peer).wait_recv()
    for peer in row_peers + [my_row]:
        side_copy(peer, peer).wait_recv()
    parts = [partials[i] for i in range(2 * n_row)]
    top = functools.reduce(jnp.maximum, parts)
    mass = functools.reduce(jnp.add, [jnp.exp(part - top) for part in parts])
    logs = top + jnp.log(mass) - pool_norms[...] * LN2
    ratio = logs[0:1, :] - logs[1:2, :]
    target_out[...] = logs[0:1, :]
    ref_out[...] = logs[1:2, :]

    local_mean = jnp.sum(ratio, axis=1, keepdims=True) / rows
    local_spread = jnp.sum(jnp.square(ratio - local_mean), axis=1, keepdims=True)
    stats[me, 0:1, :] = jnp.broadcast_to(local_mean, (1, lanes))
    stats[me, 1:2, :] = jnp.broadcast_to(local_spread, (1, lanes))

    def stat_copy(slot, peer):
        return pltpu.make_async_remote_copy(
            src_ref=stats.at[slot],
            dst_ref=stats.at[slot],
            send_sem=stat_send.at[peer],
            recv_sem=stat_recv.at[slot],
            device_id={"blk": peer},
            device_id_type=MESH,
        )

    def stat_start(i, carry):
        stat_copy(me, lax.rem(me + i, n_blk)).start()
        return carry

    def stat_wait(i, carry):
        peer = lax.rem(me + i, n_blk)
        stat_copy(peer, peer).wait_recv()
        return carry

    lax.fori_loop(1, n_blk, stat_start, 0)

    for k in range(2):

        def sent(origin, carry, k=k):
            @pl.when((origin <= place) & (place < length - 1))
            def _():
                line_copy(origin, k, gathered.at[origin, k], 1, right_send).wait_send()

            @pl.when((origin >= place) & (place > 0))
            def _():
                line_copy(origin, k, gathered.at[origin, k], -1, left_send).wait_send()

            return carry

        lax.fori_loop(0, length, sent, 0)

    def pool_sent(c, carry):
        cross_copy(c).wait_send()
        core_copy(my_row, c).wait_send()
        for peer in x_peers:
            x_copy(c, peer).wait_send()
            core_copy(peer, c).wait_send()
        return carry

    lax.fori_loop(0, CHUNKS, pool_sent, 0)
    for peer in row_peers:
        row_copy(my_row, peer).wait_send()
    for peer in row_peers + [my_row]:
        side_copy(my_row, peer).wait_send()

    lax.fori_loop(1, n_blk, stat_wait, 0)
    means = stats[:, 0, :]
    spreads = stats[:, 1, :]
    mean = jnp.sum(means, axis=0, keepdims=True) / n_blk
    spread = jnp.sum(spreads, axis=0, keepdims=True)
    spread = spread + rows * jnp.sum(jnp.square(means - mean), axis=0, keepdims=True)
    scale = jnp.sqrt(spread / (rows * n_blk) + 1e-05)
    mean_out[...] = jnp.broadcast_to(mean[:, 0:1], mean_out.shape)
    scale_out[...] = jnp.broadcast_to(scale[:, 0:1], scale_out.shape)

    def stat_sent(i, carry):
        stat_copy(me, lax.rem(me + i, n_blk)).wait_send()
        return carry

    lax.fori_loop(1, n_blk, stat_sent, 0)


def body(n_blk, n_row, pool_embeds, target_samples, reference_samples):
    rows, depth = pool_embeds.shape
    width = target_samples.shape[0]
    length = n_blk // 2
    dma = pltpu.SemaphoreType.DMA
    flops = 2 * rows * depth * 2 * width * n_blk
    log_target, log_ref, mean, scale = pl.pallas_call(
        functools.partial(density_kernel, n_blk, n_row),
        out_shape=[
            pltpu.VMEM((1, rows), jnp.float32),
            pltpu.VMEM((1, rows), jnp.float32),
            pltpu.VMEM((1, rows), jnp.float32),
            pltpu.VMEM((1, rows), jnp.float32),
        ],
        in_specs=[pl.BlockSpec(memory_space=pltpu.HBM)] * 3,
        out_specs=[pl.BlockSpec(memory_space=pltpu.VMEM)] * 4,
        scratch_shapes=[
            pltpu.VMEM((rows, depth), jnp.bfloat16),
            pltpu.VMEM((n_row, CHUNKS, rows // n_row // CHUNKS, depth), jnp.bfloat16),
            pltpu.VMEM((length, 2, width, depth), jnp.bfloat16),
            pltpu.VMEM((1, rows), jnp.float32),
            pltpu.VMEM((length, 2, width, 128), jnp.float32),
            pltpu.VMEM((4, rows), jnp.float32),
            pltpu.VMEM((4, rows), jnp.float32),
            pltpu.VMEM((2 * n_row, 2, rows), jnp.float32),
            pltpu.VMEM((2, rows), jnp.float32),
            pltpu.VMEM((n_blk, 2, 128), jnp.float32),
            dma((3,)),
            dma((length, 2)),
            dma((length, 2)),
            dma((length, 2)),
            dma((CHUNKS,)),
            dma((n_row, CHUNKS)),
            dma((n_row, CHUNKS)),
            dma((n_row, CHUNKS)),
            dma((n_row,)),
            dma((n_row,)),
            dma((2 * n_row,)),
            dma((n_blk,)),
            dma((n_blk,)),
        ],
        compiler_params=pltpu.CompilerParams(
            collective_id=0, has_side_effects=True, vmem_limit_bytes=62 * 1024 * 1024
        ),
        cost_estimate=pl.CostEstimate(flops=flops, bytes_accessed=2 * rows * depth, transcendentals=0),
    )(pool_embeds, target_samples, reference_samples)
    ratio = log_target.reshape(rows) - log_ref.reshape(rows)
    return ratio, (ratio - mean.reshape(rows)) / scale.reshape(rows)


def solution(mesh):
    in_specs = (P("blk", None), P(("blk", "row"), None), P(("blk", "row"), None))
    out_specs = (P("blk"), P("blk"))
    part = functools.partial(body, mesh.shape["blk"], mesh.shape["row"])
    return jax.shard_map(part, mesh=mesh, in_specs=in_specs, out_specs=out_specs, check_vma=False)
```

```python
import functools
import math

import jax
import jax.numpy as jnp
from jax import lax
from jax.experimental import pallas as pl
from jax.experimental.pallas import tpu as pltpu
from jax.sharding import PartitionSpec as P

KERNEL_GAIN = 30.0
LOG2E = math.log2(math.e)
LN2 = math.log(2.0)
CHUNKS = 8
MESH = pl.DeviceIdType.MESH


def density_kernel(
    n_blk,
    n_row,
    pool_hbm,
    target_hbm,
    ref_hbm,
    target_out,
    ref_out,
    mean_out,
    scale_out,
    pool,
    other_pool,
    gathered,
    pool_norms,
    sample_norms,
    high,
    total,
    partials,
    outgoing,
    stats,
    load_sem,
    right_send,
    left_send,
    line_recv,
    cross_send,
    x_send,
    core_send,
    pool_recv,
    row_send,
    side_send,
    part_recv,
    stat_send,
    stat_recv,
):
    me = lax.axis_index("blk")
    my_row = lax.axis_index("row")
    length = n_blk // 2
    place = me // 2
    other = me + 1 - 2 * lax.rem(me, 2)
    core = lax.rem(my_row, 2)
    core_peer = my_row + 1 - 2 * core
    x_peers = [lax.rem(my_row + 2 * j, n_row) for j in range(1, n_row // 2)]
    row_peers = [lax.rem(my_row + i, n_row) for i in range(1, n_row)]
    rows, depth = pool.shape
    lanes = stats.shape[2]
    width = target_hbm.shape[0]
    chunk = other_pool.shape[2]
    factor = KERNEL_GAIN / depth * LOG2E
    sources = (target_hbm, ref_hbm)
    nt = (((1,), (1,)), ((), ()))

    pool_load = pltpu.make_async_copy(pool_hbm, pool, load_sem.at[2])
    pool_load.start()
    own_loads = [
        pltpu.make_async_copy(sources[k], gathered.at[place, k], load_sem.at[k]) for k in range(2)
    ]
    for load in own_loads:
        load.start()

    barrier = pltpu.get_barrier_semaphore()

    near = pl.semaphore_signal

    @pl.when(place < length - 1)
    def _():
        near(barrier, inc=1, device_id={"blk": me + 2}, device_id_type=MESH)

    @pl.when(place > 0)
    def _():
        near(barrier, inc=1, device_id={"blk": me - 2}, device_id_type=MESH)

    near(barrier, inc=1, device_id={"blk": other}, device_id_type=MESH)
    for peer in x_peers + [core_peer]:
        near(barrier, inc=1, device_id={"row": peer}, device_id_type=MESH)
    ends = (place == 0).astype(jnp.int32) + (place == length - 1).astype(jnp.int32)
    pl.semaphore_wait(barrier, 4 + len(x_peers) - ends)

    def line_copy(origin, k, src, step, sems):
        return pltpu.make_async_remote_copy(
            src_ref=src,
            dst_ref=gathered.at[origin, k],
            send_sem=sems.at[origin, k],
            recv_sem=line_recv.at[origin, k],
            device_id={"blk": me + 2 * step},
            device_id_type=MESH,
        )

    def cross_copy(c):
        at = pl.multiple_of((my_row * CHUNKS + c) * chunk, chunk)
        return pltpu.make_async_remote_copy(
            src_ref=pool_hbm.at[pl.ds(at, chunk)],
            dst_ref=other_pool.at[my_row, c],
            send_sem=cross_send.at[c],
            recv_sem=pool_recv.at[my_row, c],
            device_id={"blk": other},
            device_id_type=MESH,
        )

    def row_relay(quarter, c, peer, send_sem):
        return pltpu.make_async_remote_copy(
            src_ref=other_pool.at[quarter, c],
            dst_ref=other_pool.at[quarter, c],
            send_sem=send_sem,
            recv_sem=pool_recv.at[quarter, c],
            device_id={"row": peer},
            device_id_type=MESH,
        )

    def core_copy(quarter, c):
        return row_relay(quarter, c, core_peer, core_send.at[quarter, c])

    def x_copy(c, peer):
        return row_relay(my_row, c, peer, x_send.at[peer, c])

    for k in range(2):

        @pl.when(place < length - 1)
        def _(k=k):
            line_copy(place, k, sources[k], 1, right_send).start()

        @pl.when(place > 0)
        def _(k=k):
            line_copy(place, k, sources[k], -1, left_send).start()

    for c in range(CHUNKS):
        cross_copy(c).start()

    high[...] = jnp.full_like(high, -1e30)
    total[...] = jnp.zeros_like(total)

    def set_norms(origin, k):
        block = gathered[origin, k].astype(jnp.float32)
        norms = jnp.sum(jnp.square(block), axis=1, keepdims=True) * factor
        sample_norms[origin, k] = jnp.broadcast_to(norms, (width, lanes))

    def fold(origin, which, count=1):
        block = gathered[pl.ds(origin, count)].reshape(count * 2 * width, depth)
        columns = pool[...] if which == 0 else other_pool[...].reshape(rows, depth)
        norms = sample_norms[pl.ds(origin, count)].reshape(count * 2 * width, lanes)
        norms = jnp.concatenate([norms] * (rows // lanes), axis=1)
        products = lax.dot_general(block, columns, nt, preferred_element_type=jnp.float32)
        scores_all = products * (2.0 * factor) - norms
        for k in range(2):
            pieces = [scores_all[(2 * j + k) * width : (2 * j + k + 1) * width, :] for j in range(count)]
            at = 2 * which + k
            old = high[at : at + 1, :]
            best = [jnp.max(piece, axis=0, keepdims=True) for piece in pieces]
            new = functools.reduce(jnp.maximum, best, old)
            sums = [jnp.sum(jnp.exp2(piece - new), axis=0, keepdims=True) for piece in pieces]
            total[at : at + 1, :] = total[at : at + 1, :] * jnp.exp2(old - new) + sum(sums)
            high[at : at + 1, :] = new

    pool_load.wait()
    for load in own_loads:
        load.wait()
    def fold_early(which):
        middle = (place > 0) & (place < length - 1)
        first = jnp.minimum(place, 1)
        if length <= 4:

            @pl.when(middle)
            def _():
                fold(0, which, length)

            @pl.when(jnp.logical_not(middle))
            def _():
                fold(first, which, length - 1)

        else:

            def early(origin, carry):
                fold(origin, which)
                return carry

            stop = first + length - 1
            lax.fori_loop(jnp.where(middle, 0, first), stop, early, 0)

    ones = jnp.ones((8, depth), jnp.bfloat16)
    tile = 256 if rows % 256 == 0 else rows

    def norm_tile(i, carry):
        at = pl.multiple_of(i * tile, tile)
        squares = jnp.square(pool[pl.ds(at, tile), :].astype(jnp.float32))
        coarse = squares.astype(jnp.bfloat16)
        fine = (squares - coarse.astype(jnp.float32)).astype(jnp.bfloat16)
        sums = lax.dot_general(ones, coarse, nt, preferred_element_type=jnp.float32)
        sums = sums + lax.dot_general(ones, fine, nt, preferred_element_type=jnp.float32)
        pool_norms[:, pl.ds(at, tile)] = sums[0:1, :] * factor
        return carry

    lax.fori_loop(0, rows // tile, norm_tile, 0)
    line_ticks = 2 * (length - 1)
    ticks = max(line_ticks, CHUNKS // 2 + 2)

    def from_side(c):
        @pl.when(c < CHUNKS)
        def _():
            cross_copy(c).wait_recv()
            for peer in x_peers:
                x_copy(c, peer).start()
            core_copy(my_row, c).start()

    def from_x(c):
        @pl.when((c >= 0) & (c < CHUNKS))
        def _():
            for peer in x_peers:
                row_relay(peer, c, peer, x_send.at[peer, c]).wait_recv()
                core_copy(peer, c).start()

    def tick(i, carry):
        step = i // 2 + 1
        k = lax.rem(i, 2)
        from_side(2 * i)

        @pl.when((i < line_ticks) & (place >= step))
        def _():
            origin = place - step
            block = gathered.at[origin, k]
            line_copy(origin, k, block, 1, right_send).wait_recv()

            @pl.when(place < length - 1)
            def _():
                line_copy(origin, k, block, 1, right_send).start()

        @pl.when((i < line_ticks) & (place + step < length))
        def _():
            origin = place + step
            block = gathered.at[origin, k]
            line_copy(origin, k, block, -1, left_send).wait_recv()

            @pl.when(place > 0)
            def _():
                line_copy(origin, k, block, -1, left_send).start()

        from_x(2 * i - 1)
        from_side(2 * i + 1)
        from_x(2 * i)

        @pl.when(i == ticks - 3)
        def _():
            def all_norms(j, carry):
                origin = j // 2

                @pl.when((origin - place < length - 1) & (place - origin < length - 1))
                def _():
                    set_norms(origin, lax.rem(j, 2))

                return carry

            lax.fori_loop(0, 2 * length, all_norms, 0)
            fold_early(0)

        @pl.when(i == ticks - 2)
        def _():
            for j in range(n_row // 2):
                quarter = lax.rem(core_peer + 2 * j, n_row)

                def arrived(c, carry, quarter=quarter):
                    core_copy(quarter, c).wait_recv()
                    return carry

                lax.fori_loop(0, CHUNKS, arrived, 0)

            fold_early(1)

        @pl.when((i >= line_ticks - 2) & (i < line_ticks) & ((place == 0) | (place == length - 1)))
        def _():
            set_norms(length - 1 - place, k)

        return carry

    lax.fori_loop(0, ticks, tick, 0)

    @pl.when((place == 0) | (place == length - 1))
    def _():
        last = length - 1 - place
        fold(last, 0)
        fold(last, 1)

    logs = (high[...] + jnp.log2(total[...])) * LN2
    partials[my_row] = logs[0:2, :]
    outgoing[...] = logs[2:4, :]

    def row_copy(slot, peer):
        return pltpu.make_async_remote_copy(
            src_ref=partials.at[slot],
            dst_ref=partials.at[slot],
            send_sem=row_send.at[peer],
            recv_sem=part_recv.at[slot],
            device_id={"row": peer},
            device_id_type=MESH,
        )

    def side_copy(row, peer):
        return pltpu.make_async_remote_copy(
            src_ref=outgoing,
            dst_ref=partials.at[n_row + row],
            send_sem=side_send.at[peer],
            recv_sem=part_recv.at[n_row + row],
            device_id={"blk": other, "row": peer},
            device_id_type=MESH,
        )

    for peer in row_peers + [my_row]:
        side_copy(my_row, peer).start()
    for peer in row_peers:
        row_copy(my_row, peer).start()
    for peer in row_peers:
        row_copy(peer, peer).wait_recv()
    for peer in row_peers + [my_row]:
        side_copy(peer, peer).wait_recv()
    parts = [partials[i] for i in range(2 * n_row)]
    top = functools.reduce(jnp.maximum, parts)
    mass = functools.reduce(jnp.add, [jnp.exp(part - top) for part in parts])
    logs = top + jnp.log(mass) - pool_norms[...] * LN2
    ratio = logs[0:1, :] - logs[1:2, :]
    target_out[...] = logs[0:1, :]
    ref_out[...] = logs[1:2, :]

    local_mean = jnp.sum(ratio, axis=1, keepdims=True) / rows
    local_spread = jnp.sum(jnp.square(ratio - local_mean), axis=1, keepdims=True)
    stats[me, 0:1, :] = jnp.broadcast_to(local_mean, (1, lanes))
    stats[me, 1:2, :] = jnp.broadcast_to(local_spread, (1, lanes))

    def stat_copy(slot, peer):
        return pltpu.make_async_remote_copy(
            src_ref=stats.at[slot],
            dst_ref=stats.at[slot],
            send_sem=stat_send.at[peer],
            recv_sem=stat_recv.at[slot],
            device_id={"blk": peer},
            device_id_type=MESH,
        )

    def stat_start(i, carry):
        stat_copy(me, lax.rem(me + i, n_blk)).start()
        return carry

    def stat_wait(i, carry):
        peer = lax.rem(me + i, n_blk)
        stat_copy(peer, peer).wait_recv()
        return carry

    lax.fori_loop(1, n_blk, stat_start, 0)

    for k in range(2):

        def sent(origin, carry, k=k):
            @pl.when((origin <= place) & (place < length - 1))
            def _():
                line_copy(origin, k, gathered.at[origin, k], 1, right_send).wait_send()

            @pl.when((origin >= place) & (place > 0))
            def _():
                line_copy(origin, k, gathered.at[origin, k], -1, left_send).wait_send()

            return carry

        lax.fori_loop(0, length, sent, 0)

    def pool_sent(c, carry):
        cross_copy(c).wait_send()
        core_copy(my_row, c).wait_send()
        for peer in x_peers:
            x_copy(c, peer).wait_send()
            core_copy(peer, c).wait_send()
        return carry

    lax.fori_loop(0, CHUNKS, pool_sent, 0)
    for peer in row_peers:
        row_copy(my_row, peer).wait_send()
    for peer in row_peers + [my_row]:
        side_copy(my_row, peer).wait_send()

    lax.fori_loop(1, n_blk, stat_wait, 0)
    means = stats[:, 0, :]
    spreads = stats[:, 1, :]
    mean = jnp.sum(means, axis=0, keepdims=True) / n_blk
    spread = jnp.sum(spreads, axis=0, keepdims=True)
    spread = spread + rows * jnp.sum(jnp.square(means - mean), axis=0, keepdims=True)
    scale = jnp.sqrt(spread / (rows * n_blk) + 1e-05)
    mean_out[...] = jnp.broadcast_to(mean[:, 0:1], mean_out.shape)
    scale_out[...] = jnp.broadcast_to(scale[:, 0:1], scale_out.shape)

    def stat_sent(i, carry):
        stat_copy(me, lax.rem(me + i, n_blk)).wait_send()
        return carry

    lax.fori_loop(1, n_blk, stat_sent, 0)


def body(n_blk, n_row, pool_embeds, target_samples, reference_samples):
    rows, depth = pool_embeds.shape
    width = target_samples.shape[0]
    length = n_blk // 2
    dma = pltpu.SemaphoreType.DMA
    flops = 2 * rows * depth * 2 * width * n_blk
    log_target, log_ref, mean, scale = pl.pallas_call(
        functools.partial(density_kernel, n_blk, n_row),
        out_shape=[
            pltpu.VMEM((1, rows), jnp.float32),
            pltpu.VMEM((1, rows), jnp.float32),
            pltpu.VMEM((1, rows), jnp.float32),
            pltpu.VMEM((1, rows), jnp.float32),
        ],
        in_specs=[pl.BlockSpec(memory_space=pltpu.HBM)] * 3,
        out_specs=[pl.BlockSpec(memory_space=pltpu.VMEM)] * 4,
        scratch_shapes=[
            pltpu.VMEM((rows, depth), jnp.bfloat16),
            pltpu.VMEM((n_row, CHUNKS, rows // n_row // CHUNKS, depth), jnp.bfloat16),
            pltpu.VMEM((length, 2, width, depth), jnp.bfloat16),
            pltpu.VMEM((1, rows), jnp.float32),
            pltpu.VMEM((length, 2, width, 128), jnp.float32),
            pltpu.VMEM((4, rows), jnp.float32),
            pltpu.VMEM((4, rows), jnp.float32),
            pltpu.VMEM((2 * n_row, 2, rows), jnp.float32),
            pltpu.VMEM((2, rows), jnp.float32),
            pltpu.VMEM((n_blk, 2, 128), jnp.float32),
            dma((3,)),
            dma((length, 2)),
            dma((length, 2)),
            dma((length, 2)),
            dma((CHUNKS,)),
            dma((n_row, CHUNKS)),
            dma((n_row, CHUNKS)),
            dma((n_row, CHUNKS)),
            dma((n_row,)),
            dma((n_row,)),
            dma((2 * n_row,)),
            dma((n_blk,)),
            dma((n_blk,)),
        ],
        compiler_params=pltpu.CompilerParams(
            collective_id=0, has_side_effects=True, vmem_limit_bytes=62 * 1024 * 1024
        ),
        cost_estimate=pl.CostEstimate(flops=flops, bytes_accessed=2 * rows * depth, transcendentals=0),
    )(pool_embeds, target_samples, reference_samples)
    ratio = log_target.reshape(rows) - log_ref.reshape(rows)
    return ratio, (ratio - mean.reshape(rows)) / scale.reshape(rows)


def solution(mesh):
    in_specs = (P("blk", None), P(("blk", "row"), None), P(("blk", "row"), None))
    out_specs = (P("blk"), P("blk"))
    part = functools.partial(body, mesh.shape["blk"], mesh.shape["row"])
    return jax.shard_map(part, mesh=mesh, in_specs=in_specs, out_specs=out_specs, check_vma=False)
```
